256 devices in a mesh: src: 8 (over z), tgt: 32 (over y, x, core).
Axes of the slice: x: 4, y: 4, z: 8, core: 2. Of those that a mesh axis runs over, the one named last changes fastest.
Arguments:
- source_latent: bfloat16 [64, 32768], P(None, 'src'), may hold values from -14 to 14
- target_latent: bfloat16 [64, 32768], P(None, 'tgt'), may hold values from -14 to 14
- source_mass: float32 [32768], P('src'), may hold values from 0.25 to 4
- target_mass: float32 [32768], P('tgt'), may hold values from 0.25 to 4
- source_region: int32 [32], P('src'), may hold values from 0 to 15, as said below
- target_region: int32 [64], P('tgt'), may hold values from 0 to 15, as said below
- allowed: int32 [16, 16], replicated, may hold values from 0 to 1, as said below
Outputs:
- source_potential: float32 [32768], P('src')
- target_potential: float32 [32768], P('tgt')
- projected: float32 [64, 32768], P('src', 'tgt')
The draws below stay inside these ranges and needn't reach their ends.
Inputs may be any that keep to these rules, and one draw needn't show every extreme that they name: `source_region`: every one of the 16 regions labels at least one source block. `target_region`: every one of the 16 regions labels at least one target block. `allowed`: the diagonal is 1.
All inputs are finite; a program needn't handle non-finite values.
Results may differ from the reference program's by a relative error of at most 0.0022.
Values sent between devices are 32-bit elements; how exact they have to be, the bound alone decides.
A program may use at most 64 MiB of HBM per device.

```python
import math
import jax
import jax.numpy as jnp
from jax import lax

K = 64
SB = 1024
TB = 512
R = 16
ITERS = 3
NS = 32768
NT = 32768


def region_labels(key, count):
    first = jnp.arange(R, dtype=jnp.int32)
    others = jax.random.randint(key, (count - R,), 0, R, dtype=jnp.int32)
    order = jax.random.permutation(jax.random.fold_in(key, 11), count)
    return jnp.concatenate([first, others])[order]


def draw_source_region(key, part):
    key = jax.random.fold_in(key, 3)
    return region_labels(key, NS // SB)


def draw_target_region(key, part):
    key = jax.random.fold_in(key, 4)
    return region_labels(key, NT // TB)


def draw_allowed(key, part):
    key = jax.random.fold_in(key, 5)
    picks = jax.random.randint(key, (R, R), 0, 4, dtype=jnp.int32)
    extra = (picks == 0).astype(jnp.int32)
    labels = jnp.arange(R, dtype=jnp.int32)
    diagonal = (labels[:, None] == labels[None, :]).astype(jnp.int32)
    return jnp.maximum(extra, diagonal)


def draw_source_latent(key, part):
    key = jax.random.fold_in(key, 1)
    normal_key = jax.random.fold_in(key, 0)
    values = jnp.clip(jax.random.normal(normal_key, (K, NS), jnp.float32), -4.0, 4.0)
    return values.astype(jnp.bfloat16)


def draw_target_latent(key, part):
    key = jax.random.fold_in(key, 2)
    normal_key = jax.random.fold_in(key, 0)
    values = jnp.clip(jax.random.normal(normal_key, (K, NT), jnp.float32), -4.0, 4.0)
    return values.astype(jnp.bfloat16)


def level_of(key, extent, cuts, smallest, high):
    def one(dim, parts):
        draws = jax.random.uniform(jax.random.fold_in(jax.random.fold_in(key, 6), dim), (parts,), jnp.float32, smallest / len(cuts), high / len(cuts))
        return jnp.repeat(jnp.exp(draws), extent[dim] // parts).reshape((-1,) + (1,) * (len(extent) - dim - 1))

    level = one(*cuts[0])
    for cut in cuts[1:]:
        level = level * one(*cut)
    return level


def setup_inputs(seed: int = 0) -> dict:
    streams_of = jax.random.split(jax.random.key(seed), 8)
    return {
        "source_latent": draw_source_latent(jax.random.fold_in(streams_of[7], 71), 0),
        "target_latent": draw_target_latent(jax.random.fold_in(streams_of[7], 71), 0),
        "source_mass": jnp.clip(jnp.exp(math.log(4.0) - 2.7725887 * jax.random.uniform(streams_of[2], (NS,), jnp.float32) ** level_of(streams_of[2], (NS,), ((0, 8),), -0.2, 0.2)), 0.25, 4.0),
        "target_mass": jnp.clip(jnp.exp(math.log(4.0) - 2.7725887 * jax.random.uniform(streams_of[3], (NT,), jnp.float32) ** level_of(streams_of[3], (NT,), ((0, 32),), -0.2, 0.2)), 0.25, 4.0),
        "source_region": draw_source_region(jax.random.fold_in(streams_of[7], 71), 0),
        "target_region": draw_target_region(jax.random.fold_in(streams_of[7], 71), 0),
        "allowed": draw_allowed(jax.random.fold_in(streams_of[7], 71), 0),
    }


ENTROPIC = 0.05
MARGINAL = 1.0
DAMPING = MARGINAL / (MARGINAL + ENTROPIC)
NEGATIVE = -1.0e30


def block_permitted(source_region, target_region, allowed):
    labels = jnp.arange(R, dtype=jnp.int32)
    row_hot = (source_region[:, None] == labels[None, :]).astype(jnp.float32)
    col_hot = (target_region[:, None] == labels[None, :]).astype(jnp.float32)
    linked = jnp.dot(jnp.dot(row_hot, allowed.astype(jnp.float32)), col_hot.T)
    return linked > 0.5


def block_distance(source_block, source_part, target_block, target_part):
    products = jnp.dot(source_block.T, target_block, preferred_element_type=jnp.float32)
    return (source_part[:, None] + target_part[None, :] - 2.0 * products) / K


def masked_lse(scores, permitted, axis):
    held = jnp.where(permitted, scores, NEGATIVE)
    largest = jnp.max(held, axis=axis, keepdims=True)
    summed = jnp.sum(jnp.where(permitted, jnp.exp(held - largest), 0.0), axis=axis)
    return jnp.squeeze(largest, axis) + jnp.log(summed)


def reference(source_latent, target_latent, source_mass, target_mass, source_region, target_region, allowed):
    source_wide = source_latent.astype(jnp.float32)
    target_wide = target_latent.astype(jnp.float32)
    source_square = jnp.sum(source_wide * source_wide, axis=0)
    target_square = jnp.sum(target_wide * target_wide, axis=0)
    source_log = jnp.log(source_mass)
    target_log = jnp.log(target_mass)
    permitted = block_permitted(source_region, target_region, allowed)
    source_count = NS // SB
    target_count = NT // TB
    source_blocks = source_latent.reshape(K, source_count, SB).transpose(1, 0, 2)
    source_square_blocks = source_square.reshape(source_count, SB)
    target_blocks = target_latent.reshape(K, target_count, TB).transpose(1, 0, 2)
    target_square_blocks = target_square.reshape(target_count, TB)

    def source_update(potential_target):
        def one_block(items):
            source_block, source_part, permit_row = items
            distance = block_distance(source_block, source_part, target_latent, target_square)
            keep_mask = jnp.repeat(permit_row, TB)[None, :]
            scores = target_log[None, :] + (potential_target[None, :] - distance) / ENTROPIC
            return -DAMPING * ENTROPIC * masked_lse(scores, keep_mask, 1)
        return lax.map(one_block, (source_blocks, source_square_blocks, permitted)).reshape(NS)

    def column_lse(potential_source):
        def one_block(items):
            target_block, target_part, permit_col = items
            distance = block_distance(source_latent, source_square, target_block, target_part)
            keep_mask = jnp.repeat(permit_col, SB)[:, None]
            scores = source_log[:, None] + (potential_source[:, None] - distance) / ENTROPIC
            return masked_lse(scores, keep_mask, 0)
        return lax.map(one_block, (target_blocks, target_square_blocks, permitted.T)).reshape(NT)

    potential_target = jnp.zeros((NT,), jnp.float32)
    potential_source = jnp.zeros((NS,), jnp.float32)
    col_lse = jnp.zeros((NT,), jnp.float32)
    for sweep_index in range(ITERS):
        potential_source = source_update(potential_target)
        col_lse = column_lse(potential_source)
        potential_target = -DAMPING * ENTROPIC * col_lse

    lse_blocks = col_lse.reshape(target_count, TB)

    def centre_block(items):
        target_block, target_part, permit_col, lse_part = items
        distance = block_distance(source_latent, source_square, target_block, target_part)
        keep_mask = jnp.repeat(permit_col, SB)[:, None]
        scores = source_log[:, None] + (potential_source[:, None] - distance) / ENTROPIC
        weights = jnp.where(keep_mask, jnp.exp(scores - lse_part[None, :]), 0.0).astype(jnp.bfloat16)
        return jnp.dot(source_latent, weights, preferred_element_type=jnp.float32)

    centred = lax.map(centre_block, (target_blocks, target_square_blocks, permitted.T, lse_blocks))
    projected = centred.transpose(1, 0, 2).reshape(K, NT)
    return potential_source, potential_target, projected
```

```python
import functools
import math

import jax
import jax.numpy as jnp
from jax import lax
from jax.experimental import pallas as pl
from jax.experimental.pallas import tpu as pltpu
from jax.sharding import PartitionSpec as P

SB = 1024
TB = 512
ITERS = 3
ENTROPIC = 0.05
MARGINAL = 1.0
DAMPING = MARGINAL / (MARGINAL + ENTROPIC)
KAPPA = math.log2(math.e) / ENTROPIC
FORBID = -(2.0**100)
MESH = pl.DeviceIdType.MESH
WIDE = 256
LANES = 128
F32 = jnp.float32
BF16 = jnp.bfloat16


def split3(value):
    high = value.astype(BF16).astype(F32)
    rest = value - high
    middle = rest.astype(BF16).astype(F32)
    return high, middle, rest - middle


def tail_rows(at, parts, ones_at):
    shape = (16, parts[0].shape[1])
    row = lax.broadcasted_iota(jnp.int32, shape, 0)
    tail = jnp.where((row >= ones_at) & (row < ones_at + 3), 1.0, 0.0)
    for offset, part in enumerate(parts):
        tail = jnp.where(row == at + offset, jnp.broadcast_to(part, shape), tail)
    return tail


def lse2(scores):
    largest = jnp.max(scores, axis=0, keepdims=True)
    summed = jnp.sum(jnp.exp2(scores - largest), axis=0, keepdims=True)
    return largest + jnp.log2(summed)


def kernel(
    xs, ys, a_mass, b_mass, s_region, t_region, allowed,
    f_out, g_out, projected,
    x_aug, y_aug, x_t, y_t, partial_row, partial_col, partial_mass,
    row_in, potential, col_in, mass_in,
    row_send, row_recv, pot_send, pot_recv, col_send, col_recv, mass_send, mass_recv,
    *, n_src, n_tgt, comm,
):
    width, n_i = xs.shape
    n_j = ys.shape[1]
    my_src = lax.axis_index("src")
    my_tgt = lax.axis_index("tgt")
    piece = n_i // n_tgt
    share = width // n_src
    src_peer = lambda r: (lax.rem(my_src + r, n_src), my_tgt)
    tgt_peer = lambda r: (my_src, lax.rem(my_tgt + r, n_tgt))

    if comm:
        barrier = pltpu.get_barrier_semaphore()

        @pl.loop(1, n_tgt)
        def _(r):
            pl.semaphore_signal(barrier, inc=1, device_id=tgt_peer(r), device_id_type=MESH)

        @pl.loop(1, n_src)
        def _(r):
            pl.semaphore_signal(barrier, inc=1, device_id=src_peer(r), device_id_type=MESH)

    x = xs[...]
    x_wide = x.astype(F32)
    y_wide = ys[...].astype(F32)
    x_term = jnp.sum(x_wide * x_wide, axis=0, keepdims=True) * (-KAPPA / width)
    y_term = jnp.sum(y_wide * y_wide, axis=0, keepdims=True) * (-KAPPA / width)
    a_log = jnp.log2(a_mass[...])
    b_log = jnp.log2(b_mass[...])
    y_parts = split3(y_wide * (2.0 * KAPPA / width))

    x_aug[0:64, :] = x
    x_aug[64:128, :] = x
    x_aug[192:256, :] = x
    row16 = lax.broadcasted_iota(jnp.int32, (16, n_i), 0)
    col16 = lax.broadcasted_iota(jnp.int32, (16, n_i), 1)
    x_aug[128:144, :] = jnp.where((row16 >= 8) & (row16 < 11), 1.0, 0.0).astype(BF16)
    x_aug[144:160, :] = jnp.where(row16 == col16 // SB, 1.0, 0.0).astype(BF16)
    x_aug[160:192, :] = jnp.zeros((32, n_i), BF16)

    y_aug[0:64, :] = y_parts[0].astype(BF16)
    y_aug[64:128, :] = y_parts[1].astype(BF16)
    y_aug[192:256, :] = y_parts[2].astype(BF16)
    row16 = lax.broadcasted_iota(jnp.int32, (16, n_j), 0)
    col16 = lax.broadcasted_iota(jnp.int32, (16, n_j), 1)
    y_aug[128:144, :] = jnp.where(row16 < 3, 1.0, 0.0).astype(BF16)
    penalty = jnp.zeros((16, n_j), F32)
    for s in range(n_i // SB):
        for t in range(n_j // TB):
            keep = allowed[s_region[s], t_region[t]]
            here = (row16 == s) & (col16 // TB == t)
            penalty = jnp.where(here, jnp.where(keep > 0, 0.0, FORBID), penalty)
    y_aug[144:160, :] = penalty.astype(BF16)
    y_aug[160:192, :] = jnp.zeros((32, n_j), BF16)

    for c in range(n_i // WIDE):
        x_t[c * WIDE : (c + 1) * WIDE, :] = x_aug[:, c * WIDE : (c + 1) * WIDE].T
    for c in range(n_j // WIDE):
        y_t[c * WIDE : (c + 1) * WIDE, :] = y_aug[:, c * WIDE : (c + 1) * WIDE].T

    if comm:
        pl.semaphore_wait(barrier, n_tgt + n_src - 2)

    b_term = b_log + y_term
    col_lse = None
    for it in range(ITERS):
        score_b = b_term if it == 0 else b_term - DAMPING * (col_lse + y_term)
        y_t[:, 128:144] = tail_rows(8, split3(score_b), 0).T.astype(BF16)

        @pl.loop(0, n_i // WIDE)
        def _(c):
            at = pl.ds(pl.multiple_of(c * WIDE, WIDE), WIDE)
            partial_row[it, :, at] = lse2(jnp.dot(y_t[...], x_aug[:, at], preferred_element_type=F32))

        if comm:

            @pl.loop(1, n_tgt)
            def _(r):
                owner = lax.rem(my_tgt + r, n_tgt)
                pltpu.make_async_remote_copy(
                    src_ref=partial_row.at[it, :, pl.ds(pl.multiple_of(owner * piece, piece), piece)],
                    dst_ref=row_in.at[it, r - 1],
                    send_sem=row_send.at[it],
                    recv_sem=row_recv.at[it],
                    device_id=(my_src, owner),
                    device_id_type=MESH,
                ).start()

        mine = pl.ds(pl.multiple_of(my_tgt * piece, piece), piece)
        own = partial_row[it, :, mine]
        if comm:
            pltpu.make_async_copy(row_in.at[it], row_in.at[it], row_recv.at[it]).wait()
            others = row_in[it]
            largest = jnp.maximum(jnp.max(others, axis=0), own)
            summed = jnp.sum(jnp.exp2(others - largest[None]), axis=0) + jnp.exp2(own - largest)
            own = largest + jnp.log2(summed)
        potential[it, :, mine] = own
        if comm:

            @pl.loop(1, n_tgt)
            def _(r):
                pltpu.make_async_remote_copy(
                    src_ref=potential.at[it, :, mine],
                    dst_ref=potential.at[it, :, mine],
                    send_sem=pot_send.at[it],
                    recv_sem=pot_recv.at[it],
                    device_id=tgt_peer(r),
                    device_id_type=MESH,
                ).start()

            rest = potential.at[it, :, pl.ds(0, n_i - piece)]
            pltpu.make_async_copy(rest, rest, pot_recv.at[it]).wait()

        f2 = -DAMPING * (potential[it] + x_term)
        if it == ITERS - 1:
            f_out[...] = f2 * (1.0 / KAPPA)
        score_a = a_log + f2 + x_term
        x_t[:, 128:144] = tail_rows(0, split3(score_a), 8).T.astype(BF16)

        @pl.loop(0, n_j // WIDE)
        def _(c):
            at = pl.ds(pl.multiple_of(c * WIDE, WIDE), WIDE)
            rhs = y_aug[:, at]
            parts = [
                lse2(jnp.dot(x_t[s * SB : (s + 1) * SB, :], rhs, preferred_element_type=F32))
                for s in range(n_i // SB)
            ]
            largest = functools.reduce(jnp.maximum, parts)
            summed = sum(jnp.exp2(part - largest) for part in parts)
            partial_col[it, :, at] = largest + jnp.log2(summed)

        col_lse = partial_col[it]
        if comm:

            @pl.loop(1, n_src)
            def _(r):
                pltpu.make_async_remote_copy(
                    src_ref=partial_col.at[it],
                    dst_ref=col_in.at[it, r - 1],
                    send_sem=col_send.at[it],
                    recv_sem=col_recv.at[it],
                    device_id=src_peer(r),
                    device_id_type=MESH,
                ).start()

            pltpu.make_async_copy(col_in.at[it], col_in.at[it], col_recv.at[it]).wait()
            others = col_in[it]
            largest = jnp.maximum(jnp.max(others, axis=0), col_lse)
            summed = jnp.sum(jnp.exp2(others - largest[None]), axis=0) + jnp.exp2(col_lse - largest)
            col_lse = largest + jnp.log2(summed)

    g_out[...] = (-DAMPING / KAPPA) * (col_lse + y_term)

    y_aug[128:144, :] = tail_rows(8, split3(-col_lse), 0).astype(BF16)

    @pl.loop(0, n_j // WIDE)
    def _(c):
        at = pl.ds(pl.multiple_of(c * WIDE, WIDE), WIDE)
        rhs = y_aug[:, at]
        total = jnp.zeros((width, WIDE), F32)
        for s in range(n_i // SB):
            scores = jnp.dot(x_t[s * SB : (s + 1) * SB, :], rhs, preferred_element_type=F32)
            weight = jnp.exp2(scores).astype(BF16)
            total += jnp.dot(xs[:, s * SB : (s + 1) * SB], weight, preferred_element_type=F32)
        for k in range(n_src):
            partial_mass[k, :, at] = total[k * share : (k + 1) * share]

    result = partial_mass[my_src]
    if comm:

        @pl.loop(1, n_src)
        def _(r):
            owner = lax.rem(my_src + r, n_src)
            pltpu.make_async_remote_copy(
                src_ref=partial_mass.at[owner],
                dst_ref=mass_in.at[r - 1],
                send_sem=mass_send,
                recv_sem=mass_recv,
                device_id=(owner, my_tgt),
                device_id_type=MESH,
            ).start()

        pltpu.make_async_copy(mass_in, mass_in, mass_recv).wait()
        result = result + jnp.sum(mass_in[...], axis=0)
    projected[...] = result

    if comm:
        for it in range(ITERS):
            pltpu.make_async_copy(row_in.at[it], row_in.at[it], row_send.at[it]).wait()
            rest = potential.at[it, :, pl.ds(0, n_i - piece)]
            pltpu.make_async_copy(rest, rest, pot_send.at[it]).wait()
            pltpu.make_async_copy(col_in.at[it], col_in.at[it], col_send.at[it]).wait()
        pltpu.make_async_copy(mass_in, mass_in, mass_send).wait()


def solution(mesh, comm=True):
    n_src, n_tgt = mesh.shape["src"], mesh.shape["tgt"]

    def per_device(xs, ys, a_mass, b_mass, s_region, t_region, allowed):
        width, n_i = xs.shape
        n_j = ys.shape[1]
        share = width // n_src
        piece = n_i // n_tgt
        vmem = pl.BlockSpec(memory_space=pltpu.VMEM)
        smem = pl.BlockSpec(memory_space=pltpu.SMEM)
        dma = pltpu.SemaphoreType.DMA
        f, g, projected = pl.pallas_call(
            functools.partial(kernel, n_src=n_src, n_tgt=n_tgt, comm=comm),
            out_shape=(
                jax.ShapeDtypeStruct((1, n_i), F32),
                jax.ShapeDtypeStruct((1, n_j), F32),
                jax.ShapeDtypeStruct((share, n_j), F32),
            ),
            in_specs=[vmem] * 4 + [smem] * 3,
            out_specs=(vmem, vmem, vmem),
            scratch_shapes=[
                pltpu.VMEM((256, n_i), BF16),
                pltpu.VMEM((256, n_j), BF16),
                pltpu.VMEM((n_i, 256), BF16),
                pltpu.VMEM((n_j, 256), BF16),
                pltpu.VMEM((ITERS, 1, n_i), F32),
                pltpu.VMEM((ITERS, 1, n_j), F32),
                pltpu.VMEM((n_src, share, n_j), F32),
                pltpu.VMEM((ITERS, n_tgt - 1, 1, piece), F32),
                pltpu.VMEM((ITERS, 1, n_i), F32),
                pltpu.VMEM((ITERS, n_src - 1, 1, n_j), F32),
                pltpu.VMEM((n_src - 1, share, n_j), F32),
                dma((ITERS,)), dma((ITERS,)), dma((ITERS,)), dma((ITERS,)),
                dma((ITERS,)), dma((ITERS,)), dma, dma,
            ],
            compiler_params=pltpu.CompilerParams(
                collective_id=0 if comm else None,
                has_side_effects=comm,
                vmem_limit_bytes=48 * 1024 * 1024,
            ),
        )(xs, ys, a_mass.reshape(1, n_i), b_mass.reshape(1, n_j), s_region, t_region, allowed)
        return f.reshape(n_i), g.reshape(n_j), projected

    placed = (P(None, "src"), P(None, "tgt"), P("src"), P("tgt"), P("src"), P("tgt"), P())
    return jax.shard_map(
        per_device,
        mesh=mesh,
        in_specs=placed,
        out_specs=(P("src"), P("tgt"), P("src", "tgt")),
        check_vma=False,
    )
```

```python
import functools
import math

import jax
import jax.numpy as jnp
from jax import lax
from jax.experimental import pallas as pl
from jax.experimental.pallas import tpu as pltpu
from jax.sharding import PartitionSpec as P

SB = 1024
TB = 512
ITERS = 3
ENTROPIC = 0.05
MARGINAL = 1.0
DAMPING = MARGINAL / (MARGINAL + ENTROPIC)
KAPPA = math.log2(math.e) / ENTROPIC
FORBID = -(2.0**100)
MESH = pl.DeviceIdType.MESH
WIDE = 256
SUB = 256
LANES = 128
TILE = 1024
TAIL = 128
F32 = jnp.float32
BF16 = jnp.bfloat16


def split3(value):
    high = value.astype(BF16).astype(F32)
    rest = value - high
    middle = rest.astype(BF16).astype(F32)
    return [high, middle, rest - middle]


def dot(a, b):
    return jnp.dot(a, b, preferred_element_type=F32)


def join(parts):
    largest = functools.reduce(jnp.maximum, parts)
    return largest + jnp.log2(sum(jnp.exp2(part - largest) for part in parts))


def lse2(scores):
    largest = jnp.max(scores, axis=0, keepdims=True)
    summed = jnp.sum(jnp.exp2(scores - largest), axis=0, keepdims=True)
    return largest, summed


def block_lse(lhs, rows, rhs):
    pairs = [lse2(dot(lhs[at : at + SUB, :], rhs)) for at in range(rows, rows + TILE, SUB)]
    largest = functools.reduce(jnp.maximum, [m for m, _ in pairs])
    summed = sum(l * jnp.exp2(m - largest) for m, l in pairs)
    return largest + jnp.log2(summed)


def gathered_lse(values):
    largest = jnp.max(values, axis=0)
    return largest + jnp.log2(jnp.sum(jnp.exp2(values - largest[None]), axis=0))


def put_potential(dense, into, first):
    stack = jnp.concatenate(split3(dense) + [jnp.zeros((8, LANES), F32)], axis=0)
    columns = stack.T
    lane = lax.broadcasted_iota(jnp.int32, columns.shape, 1)
    for block in range(8):
        own = jnp.where(lane % 8 == block, columns, 0.0)
        rows = slice(first + block * LANES, first + (block + 1) * LANES)
        into[rows, TAIL : TAIL + 24] = own[:, :24].astype(BF16)


def kernel(
    xs_hbm, ys_hbm, a_hbm, b_hbm, s_region, t_region, allowed,
    f_out, g_out, projected,
    xs, ys, a_mass, b_mass, x_aug, y_aug, x_t, y_t, x_term, y_term,
    row_in, col_parts, col_in, numer, lse_in, mass_in,
    load_sem, row_send, row_recv, col_send, col_recv, lse_send, lse_recv, mass_send, mass_recv,
    *, n_src, n_tgt, comm,
):
    width, n_i = xs.shape
    n_j = ys.shape[1]
    tiles = n_i // TILE
    chunks = n_j // WIDE
    per_tile = TILE // WIDE
    share = width // n_src
    my_src = lax.axis_index("src")
    my_tgt = lax.axis_index("tgt")

    loads = [
        pltpu.make_async_copy(source, target, load_sem.at[k])
        for k, (source, target) in enumerate(((xs_hbm, xs), (ys_hbm, ys), (a_hbm, a_mass), (b_hbm, b_mass)))
    ]
    for load in loads:
        load.start()

    if comm:
        barrier = pltpu.get_barrier_semaphore()

        @pl.loop(1, n_tgt)
        def _(r):
            peer = (my_src, lax.rem(my_tgt + r, n_tgt))
            pl.semaphore_signal(barrier, inc=1, device_id=peer, device_id_type=MESH)

        @pl.loop(1, n_src)
        def _(r):
            peer = (lax.rem(my_src + r, n_src), my_tgt)
            pl.semaphore_signal(barrier, inc=1, device_id=peer, device_id_type=MESH)

    def send(src, dst, sent, received, peer):
        pltpu.make_async_remote_copy(
            src_ref=src, dst_ref=dst, send_sem=sent, recv_sem=received, device_id=peer, device_id_type=MESH
        ).start()

    def wait(ref, sem):
        pltpu.make_async_copy(ref, ref, sem).wait()

    for load in loads:
        load.wait()

    x = xs[...]
    x_aug[0:64, :] = x
    x_aug[64:128, :] = x
    x_aug[192:256, :] = x
    row = lax.broadcasted_iota(jnp.int32, (64, n_i), 0)
    col = lax.broadcasted_iota(jnp.int32, (64, n_i), 1)
    x_aug[TAIL : TAIL + 64, :] = jnp.where((row < 24) | (row - 24 == col // SB), 1.0, 0.0).astype(BF16)
    y_wide = ys[...].astype(F32)
    y_parts = split3(y_wide * (2.0 * KAPPA / width))
    y_aug[0:64, :] = y_parts[0].astype(BF16)
    y_aug[64:128, :] = y_parts[1].astype(BF16)
    y_aug[192:256, :] = y_parts[2].astype(BF16)
    row = lax.broadcasted_iota(jnp.int32, (64, n_j), 0)
    col = lax.broadcasted_iota(jnp.int32, (64, n_j), 1)
    tail = jnp.where(row < 24, 1.0, 0.0)
    for s in range(n_i // SB):
        for t in range(n_j // TB):
            keep = allowed[s_region[s], t_region[t]]
            here = (row == 24 + s) & (col // TB == t)
            tail = jnp.where(here, jnp.where(keep > 0, 0.0, FORBID), tail)
    y_aug[TAIL : TAIL + 64, :] = tail.astype(BF16)
    for c in range(n_j // WIDE):
        y_t[c * WIDE : (c + 1) * WIDE, :] = y_aug[:, c * WIDE : (c + 1) * WIDE].T
    y_squares = jnp.sum(y_wide * y_wide, axis=0, keepdims=True) * (-KAPPA / width)
    for c in range(n_j // LANES):
        y_term[c : c + 1, :] = y_squares[:, c * LANES : (c + 1) * LANES]
    x_wide = x.astype(F32)
    x_squares = jnp.sum(x_wide * x_wide, axis=0, keepdims=True) * (-KAPPA / width)
    for c in range(n_i // LANES):
        x_term[c : c + 1, :] = x_squares[:, c * LANES : (c + 1) * LANES]
    put_potential(jnp.log2(b_mass[...]) + y_term[...], y_t, 0)

    def row_sends(it, s, which):
        if comm:
            for r in which:
                mine = row_in.at[it, s, my_tgt]
                peer = (my_src, lax.rem(my_tgt + r, n_tgt))
                send(mine, mine, row_send.at[it, s], row_recv.at[it, s], peer)

    def row_pass(it):
        per = -(-(n_tgt - 1) // per_tile)
        for s in range(tiles):
            for c in range(per_tile):
                at = s * TILE + c * WIDE
                value = block_lse(y_t, 0, x_aug[:, at : at + WIDE])
                for h in range(WIDE // LANES):
                    lane = slice(h * LANES, (h + 1) * LANES)
                    row_in[it, s, my_tgt, c * (WIDE // LANES) + h : c * (WIDE // LANES) + h + 1, :] = value[:, lane]
                if s > 0:
                    row_sends(it, s - 1, range(1 + c * per, min(n_tgt, 1 + (c + 1) * per)))
        row_sends(it, tiles - 1, range(1, n_tgt))

    def source_score(it, s):
        if comm:
            wait(row_in.at[it, s, pl.ds(0, n_tgt - 1)], row_recv.at[it, s])
        term = x_term[s * 8 : (s + 1) * 8, :]
        f2 = -DAMPING * (gathered_lse(row_in[it, s]) + term)
        put_potential(jnp.log2(a_mass[s * 8 : (s + 1) * 8, :]) + f2 + term, x_t, s * TILE)
        return f2

    def iteration(it):
        row_pass(it)

        @pl.when(it == 0)
        def _():
            for c in range(n_i // WIDE):
                x_t[c * WIDE : (c + 1) * WIDE, :] = x_aug[:, c * WIDE : (c + 1) * WIDE].T
            if comm:
                pass

        for s in range(tiles):
            source_score(it, s)
            for c in range(chunks):
                value = block_lse(x_t, s * TILE, y_aug[:, c * WIDE : (c + 1) * WIDE])
                for h in range(WIDE // LANES):
                    lane = slice(h * LANES, (h + 1) * LANES)
                    col_parts[s, c * (WIDE // LANES) + h : c * (WIDE // LANES) + h + 1, :] = value[:, lane]
        col_in[it, my_src] = join([col_parts[s] for s in range(tiles)])
        if comm:
            mine = col_in.at[it, my_src]
            for r in range(1, n_src):
                send(mine, mine, col_send.at[it], col_recv.at[it], (lax.rem(my_src + r, n_src), my_tgt))
            wait(col_in.at[it, pl.ds(0, n_src - 1)], col_recv.at[it])
        term = y_term[...]
        g2 = -DAMPING * (gathered_lse(col_in[it]) + term)
        put_potential(jnp.log2(b_mass[...]) + term + g2, y_t, 0)

    if comm:
        pl.semaphore_wait(barrier, n_tgt + n_src - 2)
    pl.loop(0, ITERS - 1)(iteration)

    last = ITERS - 1
    row_pass(last)
    largest = [None] * chunks
    summed = [None] * chunks
    for s in range(tiles):
        f_out[s * 8 : (s + 1) * 8, :] = source_score(last, s) * (1.0 / KAPPA)
        for c in range(chunks):
            at = slice(c * WIDE, (c + 1) * WIDE)
            scores = dot(x_t[s * TILE : (s + 1) * TILE, :], y_aug[:, at])
            peak = jnp.max(scores, axis=0, keepdims=True)
            if s > 0:
                peak = jnp.maximum(peak, largest[c])
                fade = jnp.exp2(largest[c] - peak)
            weight = jnp.exp2(scores - peak)
            total = jnp.sum(weight, axis=0, keepdims=True)
            product = dot(xs[:, s * TILE : (s + 1) * TILE], weight.astype(BF16))
            if s > 0:
                total += summed[c] * fade
                product += numer[:, at] * fade
            largest[c], summed[c] = peak, total
            if s < tiles - 1:
                numer[:, at] = product
                continue
            numer[:, at] = product / total
            value = peak + jnp.log2(total)
            for h in range(WIDE // LANES):
                lane = slice(h * LANES, (h + 1) * LANES)
                lse_in[my_src, c * (WIDE // LANES) + h : c * (WIDE // LANES) + h + 1, :] = value[:, lane]
            mass_in[my_src, :, at] = numer[pl.ds(pl.multiple_of(my_src * share, share), share), at]
            if comm:
                for r in range(1, n_src):
                    owner = lax.rem(my_src + r, n_src)
                    send(
                        numer.at[pl.ds(pl.multiple_of(owner * share, share), share), at],
                        mass_in.at[my_src, :, at],
                        mass_send, mass_recv, (owner, my_tgt),
                    )
    if comm:
        mine = lse_in.at[my_src]
        for r in range(1, n_src):
            send(mine, mine, lse_send, lse_recv, (lax.rem(my_src + r, n_src), my_tgt))
        wait(lse_in.at[pl.ds(0, n_src - 1)], lse_recv)
    col_lse = gathered_lse(lse_in[...])
    g_out[...] = (-DAMPING / KAPPA) * (col_lse + y_term[...])
    scale = jnp.exp2(lse_in[...] - col_lse[None])
    if comm:
        wait(mass_in.at[pl.ds(0, n_src - 1)], mass_recv)
    for c in range(n_j // LANES):
        at = slice(c * LANES, (c + 1) * LANES)
        projected[:, at] = sum(mass_in[d, :, at] * scale[d, c : c + 1, :] for d in range(n_src))

    if comm:
        for it in range(ITERS):
            for s in range(tiles):
                wait(row_in.at[it, s, pl.ds(0, n_tgt - 1)], row_send.at[it, s])
            if it < last:
                wait(col_in.at[it, pl.ds(0, n_src - 1)], col_send.at[it])
        wait(lse_in.at[pl.ds(0, n_src - 1)], lse_send)
        wait(mass_in.at[pl.ds(0, n_src - 1)], mass_send)


def solution(mesh):
    return local(mesh, mesh.shape["src"], mesh.shape["tgt"])


def local(mesh, n_src, n_tgt, comm=True):
    def per_device(xs, ys, a_mass, b_mass, s_region, t_region, allowed):
        width, n_i = xs.shape
        n_j = ys.shape[1]
        share = width // n_src
        tiles = n_i // TILE
        vmem = pl.BlockSpec(memory_space=pltpu.VMEM)
        smem = pl.BlockSpec(memory_space=pltpu.SMEM)
        hbm = pl.BlockSpec(memory_space=pltpu.HBM)
        dma = pltpu.SemaphoreType.DMA
        f, g, projected = pl.pallas_call(
            functools.partial(kernel, n_src=n_src, n_tgt=n_tgt, comm=comm),
            out_shape=(
                jax.ShapeDtypeStruct((n_i // LANES, LANES), F32),
                jax.ShapeDtypeStruct((n_j // LANES, LANES), F32),
                jax.ShapeDtypeStruct((share, n_j), F32),
            ),
            in_specs=[hbm] * 4 + [smem] * 3,
            out_specs=(vmem, vmem, vmem),
            scratch_shapes=[
                pltpu.VMEM((width, n_i), BF16),
                pltpu.VMEM((width, n_j), BF16),
                pltpu.VMEM((n_i // LANES, LANES), F32),
                pltpu.VMEM((n_j // LANES, LANES), F32),
                pltpu.VMEM((256, n_i), BF16),
                pltpu.VMEM((256, n_j), BF16),
                pltpu.VMEM((n_i, 256), BF16),
                pltpu.VMEM((n_j, 256), BF16),
                pltpu.VMEM((n_i // LANES, LANES), F32),
                pltpu.VMEM((n_j // LANES, LANES), F32),
                pltpu.VMEM((ITERS, tiles, n_tgt, 8, LANES), F32),
                pltpu.VMEM((tiles, 8, LANES), F32),
                pltpu.VMEM((ITERS, n_src, 8, LANES), F32),
                pltpu.VMEM((width, n_j), F32),
                pltpu.VMEM((n_src, 8, LANES), F32),
                pltpu.VMEM((n_src, share, n_j), F32),
                dma((4,)),
                dma((ITERS, tiles)), dma((ITERS, tiles)), dma((ITERS,)), dma((ITERS,)),
                dma, dma, dma, dma,
            ],
            compiler_params=pltpu.CompilerParams(
                collective_id=0 if comm else None,
                has_side_effects=comm,
                vmem_limit_bytes=48 * 1024 * 1024,
            ),
        )(
            xs, ys, a_mass.reshape(n_i // LANES, LANES), b_mass.reshape(n_j // LANES, LANES),
            s_region, t_region, allowed,
        )
        return f.reshape(n_i), g.reshape(n_j), projected

    placed = (P(None, "src"), P(None, "tgt"), P("src"), P("tgt"), P("src"), P("tgt"), P())
    return jax.shard_map(
        per_device,
        mesh=mesh,
        in_specs=placed,
        out_specs=(P("src"), P("tgt"), P("src", "tgt")),
        check_vma=False,
    )
```

```python
import functools
import math

import jax
import jax.numpy as jnp
from jax import lax
from jax.experimental import pallas as pl
from jax.experimental.pallas import tpu as pltpu
from jax.sharding import PartitionSpec as P

SB = 1024
TB = 512
ITERS = 3
ENTROPIC = 0.05
MARGINAL = 1.0
DAMPING = MARGINAL / (MARGINAL + ENTROPIC)
KAPPA = math.log2(math.e) / ENTROPIC
FORBID = -(2.0**100)
MESH = pl.DeviceIdType.MESH
WIDE = 256
SUB = 256
ROWS = 32
LANES = 128
TILE = 1024
TAIL = 128
POT = TAIL + 32
VMEM_MIB = 63
F32 = jnp.float32
BF16 = jnp.bfloat16


def split3(value):
    high = value.astype(BF16).astype(F32)
    rest = value - high
    middle = rest.astype(BF16).astype(F32)
    return [high, middle, rest - middle]


def dot(a, b):
    return jnp.dot(a, b, preferred_element_type=F32)


def block_lse(lhs, rhs):
    peaks, sums = [], []
    for at in range(0, lhs.shape[0], SUB):
        scores = dot(lhs[at : at + SUB, :], rhs).reshape(SUB // 8, 8, rhs.shape[1])
        peak = jnp.max(scores, axis=0)
        peaks.append(peak)
        sums.append(jnp.sum(jnp.exp2(scores - peak[None]), axis=0))
    largest = functools.reduce(jnp.maximum, peaks)
    summed = sum(total * jnp.exp2(peak - largest) for peak, total in zip(peaks, sums))
    peak = jnp.max(largest, axis=0, keepdims=True)
    return peak + jnp.log2(jnp.sum(summed * jnp.exp2(largest - peak), axis=0, keepdims=True))


def joined(values, logs):
    if not logs:
        return jnp.sum(values, axis=0)
    largest = jnp.max(values, axis=0)
    return largest + jnp.log2(jnp.sum(jnp.exp2(values - largest[None]), axis=0))


def or_nan(safe, value):
    return jnp.where(safe, value, jnp.nan)


def put_potential(dense, into):
    stack = jnp.concatenate(split3(dense) + [jnp.zeros((8, LANES), F32)], axis=0)
    columns = stack.T
    lane = lax.broadcasted_iota(jnp.int32, columns.shape, 1)
    for block in range(8):
        own = jnp.where(lane % 8 == block, columns, 0.0)
        into[block * LANES : (block + 1) * LANES, TAIL : TAIL + 24] = own[:, :24].astype(BF16)


def lane_row(dense):
    return jnp.concatenate([dense[r : r + 1, :] for r in range(8)], axis=1)


def fold_lanes(values):
    return sum(values[:, at : at + LANES] for at in range(0, values.shape[1], LANES))


def farthest_first(n_src, n_tgt):
    hops = lambda d, n: min(d, n - d)
    chips = [(r // 4, r % 4) for r in range(1, n_tgt // 2)]
    chips.sort(key=lambda o: -(hops(o[0], n_tgt // 8) + hops(o[1], 4)))
    return sorted(range(1, n_src), key=lambda r: -hops(r, n_src)), chips


def kernel(
    xs_hbm, ys_hbm, a_hbm, b_hbm, s_region, t_region, allowed,
    f_out, g_out, projected,
    ys, a_mass, b_mass, x_aug, y_aug, y_t, x_t, x_term, y_term, coupling, w_col, acc, first_f, last_f,
    pair_in, row_in, col_in, numer, numer_t, mass_in,
    load_sem, pair_send, pair_recv, row_send, row_recv, col_send, col_recv, mass_send, mass_recv,
    *, n_src, n_tgt, comm,
):
    width, n_j = ys.shape
    n_i = x_aug.shape[1]
    tiles = n_i // TILE
    chips = n_tgt // 2
    share = width // n_src
    src_order, chip_order = farthest_first(n_src, n_tgt)
    my_src = lax.axis_index("src")
    my_tgt = lax.axis_index("tgt")
    my_core = my_tgt % 2
    my_chip = my_tgt // 2
    sibling = (my_src, my_tgt + 1 - 2 * my_core)

    def chip_peer(offset):
        y = lax.rem(my_chip // 4 + offset[0], n_tgt // 8)
        return (my_src, (y * 4 + lax.rem(my_chip + offset[1], 4)) * 2 + my_core)

    def src_peer(offset):
        return (lax.rem(my_src + offset, n_src), my_tgt)

    loads = [
        pltpu.make_async_copy(source, target, load_sem.at[k])
        for k, (source, target) in enumerate((
            (ys_hbm, ys), (b_hbm, b_mass), (xs_hbm, x_aug.at[0:64]), (xs_hbm, x_aug.at[64:128]),
            (xs_hbm, x_aug.at[192:256]), (a_hbm, a_mass),
        ))
    ]
    for load in loads:
        load.start()

    if comm:
        barrier = pltpu.get_barrier_semaphore()
        peers = [sibling] + [chip_peer(o) for o in chip_order] + [src_peer(o) for o in src_order]
        for peer in peers:
            pl.semaphore_signal(barrier, inc=1, device_id=peer, device_id_type=MESH)

    def send(src, dst, sent, received, peer):
        pltpu.make_async_remote_copy(
            src_ref=src, dst_ref=dst, send_sem=sent, recv_sem=received, device_id=peer, device_id_type=MESH
        ).start()

    def wait(ref, sem):
        pltpu.make_async_copy(ref, ref, sem).wait()

    row = lax.broadcasted_iota(jnp.int32, (64, n_i), 0)
    col = lax.broadcasted_iota(jnp.int32, (64, n_i), 1)
    x_aug[TAIL : TAIL + 64, :] = jnp.where((row < 24) | (row - 24 == col // SB), 1.0, 0.0).astype(BF16)
    row = lax.broadcasted_iota(jnp.int32, (8, n_j), 0)
    col = lax.broadcasted_iota(jnp.int32, (8, n_j), 1)
    mask = jnp.zeros((8, n_j), F32)
    for s in range(n_i // SB):
        for t in range(n_j // TB):
            keep = allowed[s_region[s], t_region[t]]
            here = (row == s) & (col // TB == t)
            mask = jnp.where(here, jnp.where(keep > 0, 0.0, FORBID), mask)
    ones = jnp.where(row < 3, 1.0, 0.0)
    tail = [jnp.zeros((24, n_j), F32), mask, ones, jnp.zeros((24, n_j), F32)]
    y_aug[TAIL : TAIL + 64, :] = jnp.concatenate(tail, axis=0).astype(BF16)
    for load in loads[:2]:
        load.wait()
    y_wide = ys[...].astype(F32)
    y_parts = split3(y_wide * (2.0 * KAPPA / width))
    y_aug[0:64, :] = y_parts[0].astype(BF16)
    y_aug[64:128, :] = y_parts[1].astype(BF16)
    y_aug[192:256, :] = y_parts[2].astype(BF16)
    for c in range(n_j // WIDE):
        y_t[c * WIDE : (c + 1) * WIDE, :] = y_aug[:, c * WIDE : (c + 1) * WIDE].T
    y_squares = jnp.sum(y_wide * y_wide, axis=0, keepdims=True) * (-KAPPA / width)
    for c in range(n_j // LANES):
        y_term[c : c + 1, :] = y_squares[:, c * LANES : (c + 1) * LANES]
    b_log = jnp.log2(b_mass[...])
    put_potential(b_log + y_term[...], y_t)
    for load in loads[2:]:
        load.wait()

    def pair_send_tile(it, s):
        if comm:
            mine = pair_in.at[it, s, my_core]
            send(mine, mine, pair_send.at[it, s], pair_recv.at[it, s], sibling)

    def chip_send_tile(it, s):
        if comm:
            wait(pair_in.at[it, s, 0], pair_recv.at[it, s])
        row_in[it, s, my_chip] = joined(pair_in[it, s], it == 0)
        if comm:
            mine = row_in.at[it, s, my_chip]
            for offset in chip_order:
                send(mine, mine, row_send.at[it, s], row_recv.at[it, s], chip_peer(offset))

    def row_total(it, s):
        if comm:
            wait(row_in.at[it, s, pl.ds(0, chips - 1)], row_recv.at[it, s])
        return joined(row_in[it, s], it == 0)

    def tile_of(s):
        return slice(s * 8, (s + 1) * 8)

    def source_factor(it, s):
        total = row_total(it, s)
        a_log = jnp.log2(a_mass[tile_of(s), :])
        first = first_f[tile_of(s), :]
        f2 = -DAMPING * (jnp.log2(total) - a_log - first)
        safe = (total >= 2.0**-28) & (jnp.abs(f2 - first) <= 30.0)
        if it > 1:
            safe &= jnp.abs(f2 - last_f[tile_of(s), :]) <= 8.0
        f2 = or_nan(safe, f2)
        last_f[tile_of(s), :] = f2
        return jnp.exp2(f2 - first), f2

    def target_total(it):
        for r in range(8):
            part = jnp.sum(acc[r * LANES : (r + 1) * LANES, :].T, axis=0, keepdims=True)
            col_in[it, my_src, r : r + 1, :] = part
        if comm:
            mine = col_in.at[it, my_src]
            for offset in src_order:
                send(mine, mine, col_send.at[it], col_recv.at[it], src_peer(offset))
            wait(col_in.at[it, pl.ds(0, n_src - 1)], col_recv.at[it])
        return jnp.sum(col_in[it], axis=0)

    def target_factor(it):
        total = target_total(it)
        g2 = -DAMPING * (jnp.log2(total) - b_log)
        w = jnp.exp2(or_nan(total >= 2.0 ** (-60.0 if it == 0 else -50.0), g2))
        for r in range(8):
            w_col[r * LANES : (r + 1) * LANES, :] = jnp.broadcast_to(w[r : r + 1, :], (LANES, LANES)).T

    for s in range(tiles):
        for c in range(TILE // WIDE):
            at = s * TILE + c * WIDE
            value = block_lse(y_t, x_aug[:, at : at + WIDE])
            for h in range(WIDE // LANES):
                r = c * (WIDE // LANES) + h
                pair_in[0, s, my_core, r : r + 1, :] = value[:, h * LANES : (h + 1) * LANES]
        if comm and s == 0:
            pl.semaphore_wait(barrier, len(peers))
        pair_send_tile(0, s)
        if s > 0:
            chip_send_tile(0, s - 1)
    x_wide = x_aug[0:64, :].astype(F32)
    x_squares = jnp.sum(x_wide * x_wide, axis=0, keepdims=True) * (-KAPPA / width)
    for c in range(n_i // LANES):
        x_term[c : c + 1, :] = x_squares[:, c * LANES : (c + 1) * LANES]
    chip_send_tile(0, tiles - 1)
    for c in range(n_i // WIDE):
        x_t[c * WIDE : (c + 1) * WIDE, :] = x_aug[0:128, c * WIDE : (c + 1) * WIDE].T

    row16 = lax.broadcasted_iota(jnp.int32, (16, TILE), 0)
    for s in range(tiles):
        whole = row_total(0, s) + x_term[tile_of(s), :]
        a_log = jnp.log2(a_mass[tile_of(s), :])
        scale = a_log + (1.0 - DAMPING) * whole
        f2 = or_nan(jnp.abs(scale) <= 30.0, -DAMPING * whole)
        first_f[tile_of(s), :] = f2
        last_f[tile_of(s), :] = f2
        score = jnp.zeros((16, TILE), F32)
        for k, part in enumerate(split3(a_log + f2 + x_term[tile_of(s), :])):
            score = jnp.where(row16 == k, lane_row(part), score)
        x_aug[POT : POT + 16, s * TILE : (s + 1) * TILE] = score.astype(BF16)
        for c in range(TILE // WIDE):
            at = slice(s * TILE + c * WIDE, s * TILE + (c + 1) * WIDE)
            rhs = x_aug[:, at]
            for j in range(0, n_j, SUB):
                block = jnp.exp2(dot(y_t[j : j + SUB, :], rhs))
                coupling[j : j + SUB, at] = block
                part = fold_lanes(block)
                acc[j : j + SUB, :] = part if s == 0 and c == 0 else acc[j : j + SUB, :] + part
    target_factor(0)

    def row_sweep(it):
        for s in range(tiles):
            sums = jnp.zeros((8, TILE), F32)
            for j in range(0, n_j, ROWS):
                w = jnp.concatenate([w_col[j : j + ROWS, :]] * (TILE // LANES), axis=1)
                block = coupling[j : j + ROWS, s * TILE : (s + 1) * TILE] * w
                sums += jnp.sum(block.reshape(ROWS // 8, 8, TILE), axis=0)
            value = jnp.sum(sums, axis=0, keepdims=True)
            for r in range(8):
                pair_in[it, s, my_core, r : r + 1, :] = value[:, r * LANES : (r + 1) * LANES]
            pair_send_tile(it, s)
        for s in range(tiles):
            chip_send_tile(it, s)

    for it in range(1, ITERS - 1):
        row_sweep(it)
        for s in range(tiles):
            factor = lane_row(source_factor(it, s)[0])
            for j in range(0, n_j, ROWS):
                block = coupling[j : j + ROWS, s * TILE : (s + 1) * TILE] * factor
                part = fold_lanes(block)
                acc[j : j + ROWS, :] = part if s == 0 else acc[j : j + ROWS, :] + part
        target_factor(it)

    last = ITERS - 1
    row_sweep(last)
    for s in range(tiles):
        factor, f2 = source_factor(last, s)
        f_out[tile_of(s), :] = f2 * (1.0 / KAPPA)
        factor = lane_row(factor)
        for j in range(0, n_j, SUB):
            rows = slice(j, j + SUB)
            weight = coupling[rows, s * TILE : (s + 1) * TILE] * factor
            part = fold_lanes(weight)
            product = dot(weight.astype(BF16), x_t[s * TILE : (s + 1) * TILE, :])
            if s > 0:
                part += acc[rows, :]
                product += numer[rows, :]
            acc[rows, :] = part
            numer[rows, :] = product
            if s < tiles - 1:
                continue
            flat = product.T
            for d in range(n_src):
                numer_t[d, :, rows] = flat[d * share : (d + 1) * share, :]
            mass_in[my_src, :, rows] = numer_t[my_src, :, rows]
            if comm:
                for offset in src_order:
                    owner = lax.rem(my_src + offset, n_src)
                    send(
                        numer_t.at[owner, :, rows], mass_in.at[my_src, :, rows],
                        mass_send, mass_recv, (owner, my_tgt),
                    )
    total = target_total(last)
    g_out[...] = (-DAMPING / KAPPA) * (jnp.log2(total) - b_log)
    if comm:
        wait(mass_in.at[pl.ds(0, n_src - 1)], mass_recv)
    projected[...] = jnp.sum(mass_in[...], axis=0) / lane_row(total)

    if comm:
        for it in range(ITERS):
            for s in range(tiles):
                wait(pair_in.at[it, s, 0], pair_send.at[it, s])
                wait(row_in.at[it, s, pl.ds(0, chips - 1)], row_send.at[it, s])
            wait(col_in.at[it, pl.ds(0, n_src - 1)], col_send.at[it])
        wait(mass_in.at[pl.ds(0, n_src - 1)], mass_send)


def tail_rows(at, parts, ones_at):
    shape = (16, parts[0].shape[1])
    row = lax.broadcasted_iota(jnp.int32, shape, 0)
    tail = jnp.where((row >= ones_at) & (row < ones_at + 3), 1.0, 0.0)
    for offset, part in enumerate(parts):
        tail = jnp.where(row == at + offset, jnp.broadcast_to(part, shape), tail)
    return tail


def careful_lse(scores):
    largest = jnp.max(scores, axis=0, keepdims=True)
    summed = jnp.sum(jnp.exp2(scores - largest), axis=0, keepdims=True)
    return largest + jnp.log2(summed)


def careful_kernel(
    xs, ys, a_mass, b_mass, s_region, t_region, allowed,
    f_out, g_out, projected,
    x_aug, y_aug, x_t, y_t, partial_row, partial_col, partial_mass,
    row_in, potential, col_in, mass_in,
    row_send, row_recv, pot_send, pot_recv, col_send, col_recv, mass_send, mass_recv,
    *, n_src, n_tgt,
):
    width, n_i = xs.shape
    n_j = ys.shape[1]
    my_src = lax.axis_index("src")
    my_tgt = lax.axis_index("tgt")
    piece = n_i // n_tgt
    share = width // n_src
    src_peer = lambda r: (lax.rem(my_src + r, n_src), my_tgt)
    tgt_peer = lambda r: (my_src, lax.rem(my_tgt + r, n_tgt))

    barrier = pltpu.get_barrier_semaphore()

    @pl.loop(1, n_tgt)
    def _(r):
        pl.semaphore_signal(barrier, inc=1, device_id=tgt_peer(r), device_id_type=MESH)

    @pl.loop(1, n_src)
    def _(r):
        pl.semaphore_signal(barrier, inc=1, device_id=src_peer(r), device_id_type=MESH)

    x = xs[...]
    x_wide = x.astype(F32)
    y_wide = ys[...].astype(F32)
    x_term = jnp.sum(x_wide * x_wide, axis=0, keepdims=True) * (-KAPPA / width)
    y_term = jnp.sum(y_wide * y_wide, axis=0, keepdims=True) * (-KAPPA / width)
    a_log = jnp.log2(a_mass[...])
    b_log = jnp.log2(b_mass[...])
    y_parts = split3(y_wide * (2.0 * KAPPA / width))

    x_aug[0:64, :] = x
    x_aug[64:128, :] = x
    x_aug[192:256, :] = x
    row16 = lax.broadcasted_iota(jnp.int32, (16, n_i), 0)
    col16 = lax.broadcasted_iota(jnp.int32, (16, n_i), 1)
    x_aug[128:144, :] = jnp.where((row16 >= 8) & (row16 < 11), 1.0, 0.0).astype(BF16)
    x_aug[144:160, :] = jnp.where(row16 == col16 // SB, 1.0, 0.0).astype(BF16)
    x_aug[160:192, :] = jnp.zeros((32, n_i), BF16)

    y_aug[0:64, :] = y_parts[0].astype(BF16)
    y_aug[64:128, :] = y_parts[1].astype(BF16)
    y_aug[192:256, :] = y_parts[2].astype(BF16)
    row16 = lax.broadcasted_iota(jnp.int32, (16, n_j), 0)
    col16 = lax.broadcasted_iota(jnp.int32, (16, n_j), 1)
    y_aug[128:144, :] = jnp.where(row16 < 3, 1.0, 0.0).astype(BF16)
    penalty = jnp.zeros((16, n_j), F32)
    for s in range(n_i // SB):
        for t in range(n_j // TB):
            keep = allowed[s_region[s], t_region[t]]
            here = (row16 == s) & (col16 // TB == t)
            penalty = jnp.where(here, jnp.where(keep > 0, 0.0, FORBID), penalty)
    y_aug[144:160, :] = penalty.astype(BF16)
    y_aug[160:192, :] = jnp.zeros((32, n_j), BF16)

    for c in range(n_i // WIDE):
        x_t[c * WIDE : (c + 1) * WIDE, :] = x_aug[:, c * WIDE : (c + 1) * WIDE].T
    for c in range(n_j // WIDE):
        y_t[c * WIDE : (c + 1) * WIDE, :] = y_aug[:, c * WIDE : (c + 1) * WIDE].T

    pl.semaphore_wait(barrier, n_tgt + n_src - 2)

    b_term = b_log + y_term
    col_lse = None
    for it in range(ITERS):
        score_b = b_term if it == 0 else b_term - DAMPING * (col_lse + y_term)
        y_t[:, 128:144] = tail_rows(8, split3(score_b), 0).T.astype(BF16)

        @pl.loop(0, n_i // WIDE)
        def _(c):
            at = pl.ds(pl.multiple_of(c * WIDE, WIDE), WIDE)
            partial_row[it, :, at] = careful_lse(jnp.dot(y_t[...], x_aug[:, at], preferred_element_type=F32))


        @pl.loop(1, n_tgt)
        def _(r):
            owner = lax.rem(my_tgt + r, n_tgt)
            pltpu.make_async_remote_copy(
                src_ref=partial_row.at[it, :, pl.ds(pl.multiple_of(owner * piece, piece), piece)],
                dst_ref=row_in.at[it, r - 1],
                send_sem=row_send.at[it],
                recv_sem=row_recv.at[it],
                device_id=(my_src, owner),
                device_id_type=MESH,
            ).start()

        mine = pl.ds(pl.multiple_of(my_tgt * piece, piece), piece)
        own = partial_row[it, :, mine]
        pltpu.make_async_copy(row_in.at[it], row_in.at[it], row_recv.at[it]).wait()
        others = row_in[it]
        largest = jnp.maximum(jnp.max(others, axis=0), own)
        summed = jnp.sum(jnp.exp2(others - largest[None]), axis=0) + jnp.exp2(own - largest)
        own = largest + jnp.log2(summed)
        potential[it, :, mine] = own

        @pl.loop(1, n_tgt)
        def _(r):
            pltpu.make_async_remote_copy(
                src_ref=potential.at[it, :, mine],
                dst_ref=potential.at[it, :, mine],
                send_sem=pot_send.at[it],
                recv_sem=pot_recv.at[it],
                device_id=tgt_peer(r),
                device_id_type=MESH,
            ).start()

        rest = potential.at[it, :, pl.ds(0, n_i - piece)]
        pltpu.make_async_copy(rest, rest, pot_recv.at[it]).wait()

        f2 = -DAMPING * (potential[it] + x_term)
        if it == ITERS - 1:
            f_out[...] = f2 * (1.0 / KAPPA)
        score_a = a_log + f2 + x_term
        x_t[:, 128:144] = tail_rows(0, split3(score_a), 8).T.astype(BF16)

        @pl.loop(0, n_j // WIDE)
        def _(c):
            at = pl.ds(pl.multiple_of(c * WIDE, WIDE), WIDE)
            rhs = y_aug[:, at]
            parts = [
                careful_lse(jnp.dot(x_t[s * SB : (s + 1) * SB, :], rhs, preferred_element_type=F32))
                for s in range(n_i // SB)
            ]
            largest = functools.reduce(jnp.maximum, parts)
            summed = sum(jnp.exp2(part - largest) for part in parts)
            partial_col[it, :, at] = largest + jnp.log2(summed)

        col_lse = partial_col[it]

        @pl.loop(1, n_src)
        def _(r):
            pltpu.make_async_remote_copy(
                src_ref=partial_col.at[it],
                dst_ref=col_in.at[it, r - 1],
                send_sem=col_send.at[it],
                recv_sem=col_recv.at[it],
                device_id=src_peer(r),
                device_id_type=MESH,
            ).start()

        pltpu.make_async_copy(col_in.at[it], col_in.at[it], col_recv.at[it]).wait()
        others = col_in[it]
        largest = jnp.maximum(jnp.max(others, axis=0), col_lse)
        summed = jnp.sum(jnp.exp2(others - largest[None]), axis=0) + jnp.exp2(col_lse - largest)
        col_lse = largest + jnp.log2(summed)

    g_out[...] = (-DAMPING / KAPPA) * (col_lse + y_term)

    y_aug[128:144, :] = tail_rows(8, split3(-col_lse), 0).astype(BF16)

    @pl.loop(0, n_j // WIDE)
    def _(c):
        at = pl.ds(pl.multiple_of(c * WIDE, WIDE), WIDE)
        rhs = y_aug[:, at]
        total = jnp.zeros((width, WIDE), F32)
        for s in range(n_i // SB):
            scores = jnp.dot(x_t[s * SB : (s + 1) * SB, :], rhs, preferred_element_type=F32)
            weight = jnp.exp2(scores).astype(BF16)
            total += jnp.dot(xs[:, s * SB : (s + 1) * SB], weight, preferred_element_type=F32)
        for k in range(n_src):
            partial_mass[k, :, at] = total[k * share : (k + 1) * share]

    result = partial_mass[my_src]

    @pl.loop(1, n_src)
    def _(r):
        owner = lax.rem(my_src + r, n_src)
        pltpu.make_async_remote_copy(
            src_ref=partial_mass.at[owner],
            dst_ref=mass_in.at[r - 1],
            send_sem=mass_send,
            recv_sem=mass_recv,
            device_id=(owner, my_tgt),
            device_id_type=MESH,
        ).start()

    pltpu.make_async_copy(mass_in, mass_in, mass_recv).wait()
    result = result + jnp.sum(mass_in[...], axis=0)
    projected[...] = result

    for it in range(ITERS):
        pltpu.make_async_copy(row_in.at[it], row_in.at[it], row_send.at[it]).wait()
        rest = potential.at[it, :, pl.ds(0, n_i - piece)]
        pltpu.make_async_copy(rest, rest, pot_send.at[it]).wait()
        pltpu.make_async_copy(col_in.at[it], col_in.at[it], col_send.at[it]).wait()
    pltpu.make_async_copy(mass_in, mass_in, mass_send).wait()


def solution(mesh):
    return local(mesh, mesh.shape["src"], mesh.shape["tgt"])


def local(mesh, n_src, n_tgt, comm=True):
    def per_device(xs, ys, a_mass, b_mass, s_region, t_region, allowed):
        width, n_i = xs.shape
        n_j = ys.shape[1]
        share = width // n_src
        tiles = n_i // TILE
        chips = n_tgt // 2
        piece = n_i // n_tgt
        vmem = pl.BlockSpec(memory_space=pltpu.VMEM)
        smem = pl.BlockSpec(memory_space=pltpu.SMEM)
        hbm = pl.BlockSpec(memory_space=pltpu.HBM)
        dma = pltpu.SemaphoreType.DMA

        def call(body, in_hbm, f_shape, g_shape, scratch, identity):
            return pl.pallas_call(
                functools.partial(body, n_src=n_src, n_tgt=n_tgt),
                out_shape=(
                    jax.ShapeDtypeStruct(f_shape, F32),
                    jax.ShapeDtypeStruct(g_shape, F32),
                    jax.ShapeDtypeStruct((share, n_j), F32),
                ),
                in_specs=[hbm if in_hbm else vmem] * 4 + [smem] * 3,
                out_specs=(vmem, vmem, vmem),
                scratch_shapes=scratch,
                compiler_params=pltpu.CompilerParams(
                    collective_id=identity if comm else None,
                    has_side_effects=comm,
                    vmem_limit_bytes=VMEM_MIB * 1024 * 1024,
                ),
            )(xs, ys, a_mass.reshape(f_shape), b_mass.reshape(g_shape), s_region, t_region, allowed)

        f, g, projected = call(
            functools.partial(kernel, comm=comm), True, (n_i // LANES, LANES), (n_j // LANES, LANES),
            [
                pltpu.VMEM((width, n_j), BF16),
                pltpu.VMEM((n_i // LANES, LANES), F32),
                pltpu.VMEM((n_j // LANES, LANES), F32),
                pltpu.VMEM((256, n_i), BF16),
                pltpu.VMEM((256, n_j), BF16),
                pltpu.VMEM((n_j, 256), BF16),
                pltpu.VMEM((n_i, 128), BF16),
                pltpu.VMEM((n_i // LANES, LANES), F32),
                pltpu.VMEM((n_j // LANES, LANES), F32),
                pltpu.VMEM((n_j, n_i), F32),
                pltpu.VMEM((n_j, LANES), F32),
                pltpu.VMEM((n_j, LANES), F32),
                pltpu.VMEM((n_i // LANES, LANES), F32),
                pltpu.VMEM((n_i // LANES, LANES), F32),
                pltpu.VMEM((ITERS, tiles, 2, 8, LANES), F32),
                pltpu.VMEM((ITERS, tiles, chips, 8, LANES), F32),
                pltpu.VMEM((ITERS, n_src, 8, LANES), F32),
                pltpu.VMEM((n_j, LANES), F32),
                pltpu.VMEM((n_src, share, n_j), F32),
                pltpu.VMEM((n_src, share, n_j), F32),
                dma((6,)),
                dma((ITERS, tiles)), dma((ITERS, tiles)), dma((ITERS, tiles)), dma((ITERS, tiles)),
                dma((ITERS,)), dma((ITERS,)), dma, dma,
            ],
            0,
        )
        f, g = f.reshape(n_i), g.reshape(n_j)
        if not comm:
            return f, g, projected

        def careful():
            f, g, projected = call(
                careful_kernel, False, (1, n_i), (1, n_j),
                [
                    pltpu.VMEM((256, n_i), BF16),
                    pltpu.VMEM((256, n_j), BF16),
                    pltpu.VMEM((n_i, 256), BF16),
                    pltpu.VMEM((n_j, 256), BF16),
                    pltpu.VMEM((ITERS, 1, n_i), F32),
                    pltpu.VMEM((ITERS, 1, n_j), F32),
                    pltpu.VMEM((n_src, share, n_j), F32),
                    pltpu.VMEM((ITERS, n_tgt - 1, 1, piece), F32),
                    pltpu.VMEM((ITERS, 1, n_i), F32),
                    pltpu.VMEM((ITERS, n_src - 1, 1, n_j), F32),
                    pltpu.VMEM((n_src - 1, share, n_j), F32),
                    dma((ITERS,)), dma((ITERS,)), dma((ITERS,)), dma((ITERS,)),
                    dma((ITERS,)), dma((ITERS,)), dma, dma,
                ],
                1,
            )
            return f.reshape(n_i), g.reshape(n_j), projected

        return lax.cond(jnp.isnan(g[0]), careful, lambda: (f, g, projected))

    placed = (P(None, "src"), P(None, "tgt"), P("src"), P("tgt"), P("src"), P("tgt"), P())
    return jax.shard_map(
        per_device,
        mesh=mesh,
        in_specs=placed,
        out_specs=(P("src"), P("tgt"), P("src", "tgt")),
        check_vma=False,
    )
```

```python
import functools
import math

import jax
import jax.numpy as jnp
from jax import lax
from jax.experimental import pallas as pl
from jax.experimental.pallas import tpu as pltpu
from jax.sharding import PartitionSpec as P

SB = 1024
TB = 512
ITERS = 3
ENTROPIC = 0.05
MARGINAL = 1.0
DAMPING = MARGINAL / (MARGINAL + ENTROPIC)
KAPPA = math.log2(math.e) / ENTROPIC
FORBID = -(2.0**100)
MESH = pl.DeviceIdType.MESH
WIDE = 256
SUB = 256
ROWS = 32
LANES = 128
TILE = 1024
TAIL = 128
POT = TAIL + 32
VMEM_MIB = 63
SHIFT = 60.0
LARGEST = 2.0**110
F32 = jnp.float32
BF16 = jnp.bfloat16


def split3(value):
    high = value.astype(BF16).astype(F32)
    rest = value - high
    middle = rest.astype(BF16).astype(F32)
    return [high, middle, rest - middle]


def dot(a, b):
    return jnp.dot(a, b, preferred_element_type=F32)


def or_nan(safe, value):
    return jnp.where(safe, value, jnp.nan)


def put_potential(dense, into):
    stack = jnp.concatenate(split3(dense) + [jnp.zeros((8, LANES), F32)], axis=0)
    columns = stack.T
    lane = lax.broadcasted_iota(jnp.int32, columns.shape, 1)
    for block in range(8):
        own = jnp.where(lane % 8 == block, columns, 0.0)
        into[block * LANES : (block + 1) * LANES, TAIL : TAIL + 24] = own[:, :24].astype(BF16)


def lane_row(dense):
    return jnp.concatenate([dense[r : r + 1, :] for r in range(8)], axis=1)


def fold_lanes(values):
    return sum(values[:, at : at + LANES] for at in range(0, values.shape[1], LANES))


def farthest_first(n_src, n_tgt):
    hops = lambda d, n: min(d, n - d)
    chips = [(r // 4, r % 4) for r in range(1, n_tgt // 2)]
    chips.sort(key=lambda o: -(hops(o[0], n_tgt // 8) + hops(o[1], 4)))
    return sorted(range(1, n_src), key=lambda r: -hops(r, n_src)), chips


def kernel(
    xs_hbm, ys_hbm, a_hbm, b_hbm, s_hbm, t_hbm, allowed_hbm,
    f_out, g_out, projected, b_copy, failed, s_copy, t_copy,
    ys, a_mass, b_mass, s_region, t_region, allowed, x_aug, y_aug, y_t, x_t, y_term, coupling, w_col, acc, last_f,
    pair_in, row_in, col_in, numer, numer_t, mass_in,
    load_sem, pair_send, pair_recv, row_send, row_recv, col_send, col_recv, mass_send, mass_recv,
    *, n_src, n_tgt, comm,
):
    width, n_j = ys.shape
    n_i = x_aug.shape[1]
    tiles = n_i // TILE
    chips = n_tgt // 2
    share = width // n_src
    src_order, chip_order = farthest_first(n_src, n_tgt)
    my_src = lax.axis_index("src")
    my_tgt = lax.axis_index("tgt")
    my_core = my_tgt % 2
    my_chip = my_tgt // 2
    sibling = (my_src, my_tgt + 1 - 2 * my_core)

    def chip_peer(offset):
        y = lax.rem(my_chip // 4 + offset[0], n_tgt // 8)
        return (my_src, (y * 4 + lax.rem(my_chip + offset[1], 4)) * 2 + my_core)

    def src_peer(offset):
        return (lax.rem(my_src + offset, n_src), my_tgt)

    loads = [
        pltpu.make_async_copy(source, target, load_sem.at[k])
        for k, (source, target) in enumerate((
            (ys_hbm, ys), (b_hbm, b_mass), (xs_hbm, x_aug.at[0:64]), (xs_hbm, x_aug.at[64:128]),
            (xs_hbm, x_aug.at[192:256]), (a_hbm, a_mass), (s_hbm, s_region), (t_hbm, t_region), (allowed_hbm, allowed),
        ))
    ]
    for load in loads:
        load.start()

    if comm:
        barrier = pltpu.get_barrier_semaphore()
        peers = [sibling] + [chip_peer(o) for o in chip_order] + [src_peer(o) for o in src_order]
        for peer in peers:
            pl.semaphore_signal(barrier, inc=1, device_id=peer, device_id_type=MESH)

    def send(src, dst, sent, received, peer):
        pltpu.make_async_remote_copy(
            src_ref=src, dst_ref=dst, send_sem=sent, recv_sem=received, device_id=peer, device_id_type=MESH
        ).start()

    def wait(ref, sem):
        pltpu.make_async_copy(ref, ref, sem).wait()

    row = lax.broadcasted_iota(jnp.int32, (32, n_i), 0)
    col = lax.broadcasted_iota(jnp.int32, (32, n_i), 1)
    x_aug[TAIL:POT, :] = jnp.where((row < 24) | (row - 24 == col // SB), 1.0, 0.0).astype(BF16)
    x_aug[POT + 16 : POT + 32, :] = jnp.zeros((16, n_i), BF16)
    for load in loads[:2] + loads[6:]:
        load.wait()
    row = lax.broadcasted_iota(jnp.int32, (8, n_j), 0)
    col = lax.broadcasted_iota(jnp.int32, (8, n_j), 1)
    mask = jnp.zeros((8, n_j), F32)
    for s in range(n_i // SB):
        for t in range(n_j // TB):
            keep = allowed[s_region[s], t_region[t]]
            here = (row == s) & (col // TB == t)
            mask = jnp.where(here, jnp.where(keep > 0, 0.0, FORBID), mask)
    ones = jnp.where(row < 3, 1.0, 0.0)
    tail = [jnp.zeros((24, n_j), F32), mask, ones, jnp.zeros((24, n_j), F32)]
    y_aug[TAIL : TAIL + 64, :] = jnp.concatenate(tail, axis=0).astype(BF16)
    y_wide = ys[...].astype(F32)
    y_parts = split3(y_wide * (2.0 * KAPPA / width))
    y_aug[0:64, :] = y_parts[0].astype(BF16)
    y_aug[64:128, :] = y_parts[1].astype(BF16)
    y_aug[192:256, :] = y_parts[2].astype(BF16)
    for c in range(n_j // WIDE):
        y_t[c * WIDE : (c + 1) * WIDE, :] = y_aug[:, c * WIDE : (c + 1) * WIDE].T
    y_squares = jnp.sum(y_wide * y_wide, axis=0, keepdims=True) * (-KAPPA / width)
    for c in range(n_j // LANES):
        y_term[c : c + 1, :] = y_squares[:, c * LANES : (c + 1) * LANES]
    b_log = jnp.log2(b_mass[...])
    put_potential(b_log + y_term[...] + SHIFT, y_t)
    for load in loads[2:6]:
        load.wait()
    row16 = lax.broadcasted_iota(jnp.int32, (16, TILE), 0)
    for s in range(tiles):
        at = slice(s * TILE, (s + 1) * TILE)
        x_wide = x_aug[0:64, at].astype(F32)
        x_term = jnp.sum(x_wide * x_wide, axis=0, keepdims=True) * (-KAPPA / width)
        tail = jnp.zeros((16, TILE), F32)
        for k, part in enumerate(split3(x_term)):
            tail = jnp.where(row16 == k, part, tail)
        x_aug[POT : POT + 16, at] = tail.astype(BF16)

    def pair_send_tile(it, s):
        if comm:
            mine = pair_in.at[it, s, my_core]
            send(mine, mine, pair_send.at[it, s], pair_recv.at[it, s], sibling)

    def chip_send_tile(it, s):
        if comm:
            wait(pair_in.at[it, s, 0], pair_recv.at[it, s])
        row_in[it, s, my_chip] = pair_in[it, s, 0] + pair_in[it, s, 1]
        if comm:
            mine = row_in.at[it, s, my_chip]
            for offset in chip_order:
                send(mine, mine, row_send.at[it, s], row_recv.at[it, s], chip_peer(offset))

    def row_total(it, s):
        if comm:
            wait(row_in.at[it, s, pl.ds(0, chips - 1)], row_recv.at[it, s])
        return jnp.sum(row_in[it, s], axis=0)

    def tile_of(s):
        return slice(s * 8, (s + 1) * 8)

    def source_factor(it, s):
        total = row_total(it, s)
        f2 = -DAMPING * (jnp.log2(total) - SHIFT)
        safe = (total >= 2.0 ** (SHIFT - 95.0)) & (total <= LARGEST)
        if it == ITERS - 1:
            safe &= jnp.abs(f2 - last_f[tile_of(s), :]) <= 8.0
        f2 = or_nan(safe, f2)
        last_f[tile_of(s), :] = f2
        return jnp.exp2(f2 + jnp.log2(a_mass[tile_of(s), :])), f2

    def target_total(it):
        for r in range(8):
            part = jnp.sum(acc[r * LANES : (r + 1) * LANES, :].T, axis=0, keepdims=True)
            col_in[it, my_src, r : r + 1, :] = part
        if comm:
            mine = col_in.at[it, my_src]
            for offset in src_order:
                send(mine, mine, col_send.at[it], col_recv.at[it], src_peer(offset))
            wait(col_in.at[it, pl.ds(0, n_src - 1)], col_recv.at[it])
        return jnp.sum(col_in[it], axis=0)

    def target_potential(total):
        return -DAMPING * (jnp.log2(total) - SHIFT - b_log)

    def target_factor(it):
        total = target_total(it)
        safe = (total >= 2.0 ** (SHIFT - 49.0)) & (total <= LARGEST)
        w = jnp.exp2(or_nan(safe, target_potential(total)))
        for r in range(8):
            w_col[r * LANES : (r + 1) * LANES, :] = jnp.broadcast_to(w[r : r + 1, :], (LANES, LANES)).T

    for s in range(tiles):
        for c in range(TILE // WIDE):
            at = slice(s * TILE + c * WIDE, s * TILE + (c + 1) * WIDE)
            rhs = x_aug[:, at]
            sums = jnp.zeros((8, WIDE), F32)
            for j in range(0, n_j, SUB):
                block = jnp.exp2(dot(y_t[j : j + SUB, :], rhs))
                coupling[j : j + SUB, at] = block
                sums += jnp.sum(block.reshape(SUB // 8, 8, WIDE), axis=0)
            value = jnp.sum(sums, axis=0, keepdims=True)
            for h in range(WIDE // LANES):
                r = c * (WIDE // LANES) + h
                pair_in[0, s, my_core, r : r + 1, :] = value[:, h * LANES : (h + 1) * LANES]
        if comm and s == 0:
            pl.semaphore_wait(barrier, len(peers))
        pair_send_tile(0, s)
        if s > 0:
            chip_send_tile(0, s - 1)
    chip_send_tile(0, tiles - 1)
    for c in range(n_i // WIDE):
        x_t[c * WIDE : (c + 1) * WIDE, :] = x_aug[0:128, c * WIDE : (c + 1) * WIDE].T

    def row_sweep(it):
        for s in range(tiles):
            sums = jnp.zeros((8, TILE), F32)
            for j in range(0, n_j, ROWS):
                w = jnp.concatenate([w_col[j : j + ROWS, :]] * (TILE // LANES), axis=1)
                block = coupling[j : j + ROWS, s * TILE : (s + 1) * TILE] * w
                sums += jnp.sum(block.reshape(ROWS // 8, 8, TILE), axis=0)
            value = jnp.sum(sums, axis=0, keepdims=True)
            for r in range(8):
                pair_in[it, s, my_core, r : r + 1, :] = value[:, r * LANES : (r + 1) * LANES]
            pair_send_tile(it, s)
            if s > 1:
                chip_send_tile(it, s - 2)
        for s in range(tiles - 2, tiles):
            chip_send_tile(it, s)

    for it in range(ITERS - 1):
        if it > 0:
            row_sweep(it)
        for s in range(tiles):
            factor = lane_row(source_factor(it, s)[0])
            for j in range(0, n_j, ROWS):
                block = coupling[j : j + ROWS, s * TILE : (s + 1) * TILE] * factor
                part = fold_lanes(block)
                acc[j : j + ROWS, :] = part if s == 0 else acc[j : j + ROWS, :] + part
        target_factor(it)

    last = ITERS - 1
    row_sweep(last)
    for s in range(tiles):
        factor, f2 = source_factor(last, s)
        f_out[tile_of(s), :] = f2 * (1.0 / KAPPA)
        factor = lane_row(factor)
        for j in range(0, n_j, SUB):
            rows = slice(j, j + SUB)
            weight = coupling[rows, s * TILE : (s + 1) * TILE] * factor
            part = fold_lanes(weight)
            latent = x_t[s * TILE : (s + 1) * TILE, :]
            product = dot(weight.astype(BF16), latent)
            if s > 0:
                part += acc[rows, :]
                product += numer[rows, :]
            acc[rows, :] = part
            numer[rows, :] = product
            if s < tiles - 1:
                continue
            flat = product.T
            for d in range(n_src):
                numer_t[d, :, rows] = flat[d * share : (d + 1) * share, :]
            mass_in[my_src, :, rows] = numer_t[my_src, :, rows]
            if comm:
                for offset in src_order:
                    owner = lax.rem(my_src + offset, n_src)
                    send(
                        numer_t.at[owner, :, rows], mass_in.at[my_src, :, rows],
                        mass_send, mass_recv, (owner, my_tgt),
                    )
    total = target_total(last)
    g2 = target_potential(total)
    g_out[...] = g2 * (1.0 / KAPPA)
    for k in range(n_i // SB):
        s_copy[k] = s_region[k]
    for k in range(n_j // TB):
        t_copy[k] = t_region[k]
    b_copy[...] = b_mass[...]
    failed[0] = jnp.sum(jnp.where(g2 == g2, 0, 1))
    if comm:
        wait(mass_in.at[pl.ds(0, n_src - 1)], mass_recv)
    projected[...] = jnp.sum(mass_in[...], axis=0) / lane_row(total)

    if comm:
        for it in range(ITERS):
            for s in range(tiles):
                wait(pair_in.at[it, s, 0], pair_send.at[it, s])
                wait(row_in.at[it, s, pl.ds(0, chips - 1)], row_send.at[it, s])
            wait(col_in.at[it, pl.ds(0, n_src - 1)], col_send.at[it])
        wait(mass_in.at[pl.ds(0, n_src - 1)], mass_send)


def tail_rows(at, parts, ones_at):
    shape = (16, parts[0].shape[1])
    row = lax.broadcasted_iota(jnp.int32, shape, 0)
    tail = jnp.where((row >= ones_at) & (row < ones_at + 3), 1.0, 0.0)
    for offset, part in enumerate(parts):
        tail = jnp.where(row == at + offset, jnp.broadcast_to(part, shape), tail)
    return tail


def careful_lse(scores):
    largest = jnp.max(scores, axis=0, keepdims=True)
    summed = jnp.sum(jnp.exp2(scores - largest), axis=0, keepdims=True)
    return largest + jnp.log2(summed)


def careful_kernel(
    xs, ys, a_mass, b_mass, s_region, t_region, allowed,
    f_out, g_out, projected,
    x_aug, y_aug, x_t, y_t, partial_row, partial_col, partial_mass,
    row_in, potential, col_in, mass_in,
    row_send, row_recv, pot_send, pot_recv, col_send, col_recv, mass_send, mass_recv,
    *, n_src, n_tgt,
):
    width, n_i = xs.shape
    n_j = ys.shape[1]
    my_src = lax.axis_index("src")
    my_tgt = lax.axis_index("tgt")
    piece = n_i // n_tgt
    share = width // n_src
    src_peer = lambda r: (lax.rem(my_src + r, n_src), my_tgt)
    tgt_peer = lambda r: (my_src, lax.rem(my_tgt + r, n_tgt))

    barrier = pltpu.get_barrier_semaphore()

    @pl.loop(1, n_tgt)
    def _(r):
        pl.semaphore_signal(barrier, inc=1, device_id=tgt_peer(r), device_id_type=MESH)

    @pl.loop(1, n_src)
    def _(r):
        pl.semaphore_signal(barrier, inc=1, device_id=src_peer(r), device_id_type=MESH)

    x = xs[...]
    x_wide = x.astype(F32)
    y_wide = ys[...].astype(F32)
    x_term = jnp.sum(x_wide * x_wide, axis=0, keepdims=True) * (-KAPPA / width)
    y_term = jnp.sum(y_wide * y_wide, axis=0, keepdims=True) * (-KAPPA / width)
    a_log = jnp.log2(a_mass[...])
    b_log = jnp.log2(b_mass[...])
    y_parts = split3(y_wide * (2.0 * KAPPA / width))

    x_aug[0:64, :] = x
    x_aug[64:128, :] = x
    x_aug[192:256, :] = x
    row16 = lax.broadcasted_iota(jnp.int32, (16, n_i), 0)
    col16 = lax.broadcasted_iota(jnp.int32, (16, n_i), 1)
    x_aug[128:144, :] = jnp.where((row16 >= 8) & (row16 < 11), 1.0, 0.0).astype(BF16)
    x_aug[144:160, :] = jnp.where(row16 == col16 // SB, 1.0, 0.0).astype(BF16)
    x_aug[160:192, :] = jnp.zeros((32, n_i), BF16)

    y_aug[0:64, :] = y_parts[0].astype(BF16)
    y_aug[64:128, :] = y_parts[1].astype(BF16)
    y_aug[192:256, :] = y_parts[2].astype(BF16)
    row16 = lax.broadcasted_iota(jnp.int32, (16, n_j), 0)
    col16 = lax.broadcasted_iota(jnp.int32, (16, n_j), 1)
    y_aug[128:144, :] = jnp.where(row16 < 3, 1.0, 0.0).astype(BF16)
    penalty = jnp.zeros((16, n_j), F32)
    for s in range(n_i // SB):
        for t in range(n_j // TB):
            keep = allowed[s_region[s], t_region[t]]
            here = (row16 == s) & (col16 // TB == t)
            penalty = jnp.where(here, jnp.where(keep > 0, 0.0, FORBID), penalty)
    y_aug[144:160, :] = penalty.astype(BF16)
    y_aug[160:192, :] = jnp.zeros((32, n_j), BF16)

    for c in range(n_i // WIDE):
        x_t[c * WIDE : (c + 1) * WIDE, :] = x_aug[:, c * WIDE : (c + 1) * WIDE].T
    for c in range(n_j // WIDE):
        y_t[c * WIDE : (c + 1) * WIDE, :] = y_aug[:, c * WIDE : (c + 1) * WIDE].T

    pl.semaphore_wait(barrier, n_tgt + n_src - 2)

    b_term = b_log + y_term
    col_lse = None
    for it in range(ITERS):
        score_b = b_term if it == 0 else b_term - DAMPING * (col_lse + y_term)
        y_t[:, 128:144] = tail_rows(8, split3(score_b), 0).T.astype(BF16)

        @pl.loop(0, n_i // WIDE)
        def _(c):
            at = pl.ds(pl.multiple_of(c * WIDE, WIDE), WIDE)
            partial_row[it, :, at] = careful_lse(jnp.dot(y_t[...], x_aug[:, at], preferred_element_type=F32))


        @pl.loop(1, n_tgt)
        def _(r):
            owner = lax.rem(my_tgt + r, n_tgt)
            pltpu.make_async_remote_copy(
                src_ref=partial_row.at[it, :, pl.ds(pl.multiple_of(owner * piece, piece), piece)],
                dst_ref=row_in.at[it, r - 1],
                send_sem=row_send.at[it],
                recv_sem=row_recv.at[it],
                device_id=(my_src, owner),
                device_id_type=MESH,
            ).start()

        mine = pl.ds(pl.multiple_of(my_tgt * piece, piece), piece)
        own = partial_row[it, :, mine]
        pltpu.make_async_copy(row_in.at[it], row_in.at[it], row_recv.at[it]).wait()
        others = row_in[it]
        largest = jnp.maximum(jnp.max(others, axis=0), own)
        summed = jnp.sum(jnp.exp2(others - largest[None]), axis=0) + jnp.exp2(own - largest)
        own = largest + jnp.log2(summed)
        potential[it, :, mine] = own

        @pl.loop(1, n_tgt)
        def _(r):
            pltpu.make_async_remote_copy(
                src_ref=potential.at[it, :, mine],
                dst_ref=potential.at[it, :, mine],
                send_sem=pot_send.at[it],
                recv_sem=pot_recv.at[it],
                device_id=tgt_peer(r),
                device_id_type=MESH,
            ).start()

        rest = potential.at[it, :, pl.ds(0, n_i - piece)]
        pltpu.make_async_copy(rest, rest, pot_recv.at[it]).wait()

        f2 = -DAMPING * (potential[it] + x_term)
        if it == ITERS - 1:
            f_out[...] = f2 * (1.0 / KAPPA)
        score_a = a_log + f2 + x_term
        x_t[:, 128:144] = tail_rows(0, split3(score_a), 8).T.astype(BF16)

        @pl.loop(0, n_j // WIDE)
        def _(c):
            at = pl.ds(pl.multiple_of(c * WIDE, WIDE), WIDE)
            rhs = y_aug[:, at]
            parts = [
                careful_lse(jnp.dot(x_t[s * SB : (s + 1) * SB, :], rhs, preferred_element_type=F32))
                for s in range(n_i // SB)
            ]
            largest = functools.reduce(jnp.maximum, parts)
            summed = sum(jnp.exp2(part - largest) for part in parts)
            partial_col[it, :, at] = largest + jnp.log2(summed)

        col_lse = partial_col[it]

        @pl.loop(1, n_src)
        def _(r):
            pltpu.make_async_remote_copy(
                src_ref=partial_col.at[it],
                dst_ref=col_in.at[it, r - 1],
                send_sem=col_send.at[it],
                recv_sem=col_recv.at[it],
                device_id=src_peer(r),
                device_id_type=MESH,
            ).start()

        pltpu.make_async_copy(col_in.at[it], col_in.at[it], col_recv.at[it]).wait()
        others = col_in[it]
        largest = jnp.maximum(jnp.max(others, axis=0), col_lse)
        summed = jnp.sum(jnp.exp2(others - largest[None]), axis=0) + jnp.exp2(col_lse - largest)
        col_lse = largest + jnp.log2(summed)

    g_out[...] = (-DAMPING / KAPPA) * (col_lse + y_term)

    y_aug[128:144, :] = tail_rows(8, split3(-col_lse), 0).astype(BF16)

    @pl.loop(0, n_j // WIDE)
    def _(c):
        at = pl.ds(pl.multiple_of(c * WIDE, WIDE), WIDE)
        rhs = y_aug[:, at]
        total = jnp.zeros((width, WIDE), F32)
        for s in range(n_i // SB):
            scores = jnp.dot(x_t[s * SB : (s + 1) * SB, :], rhs, preferred_element_type=F32)
            weight = jnp.exp2(scores).astype(BF16)
            total += jnp.dot(xs[:, s * SB : (s + 1) * SB], weight, preferred_element_type=F32)
        for k in range(n_src):
            partial_mass[k, :, at] = total[k * share : (k + 1) * share]

    result = partial_mass[my_src]

    @pl.loop(1, n_src)
    def _(r):
        owner = lax.rem(my_src + r, n_src)
        pltpu.make_async_remote_copy(
            src_ref=partial_mass.at[owner],
            dst_ref=mass_in.at[r - 1],
            send_sem=mass_send,
            recv_sem=mass_recv,
            device_id=(owner, my_tgt),
            device_id_type=MESH,
        ).start()

    pltpu.make_async_copy(mass_in, mass_in, mass_recv).wait()
    result = result + jnp.sum(mass_in[...], axis=0)
    projected[...] = result

    for it in range(ITERS):
        pltpu.make_async_copy(row_in.at[it], row_in.at[it], row_send.at[it]).wait()
        rest = potential.at[it, :, pl.ds(0, n_i - piece)]
        pltpu.make_async_copy(rest, rest, pot_send.at[it]).wait()
        pltpu.make_async_copy(col_in.at[it], col_in.at[it], col_send.at[it]).wait()
    pltpu.make_async_copy(mass_in, mass_in, mass_send).wait()


def solution(mesh):
    return local(mesh, mesh.shape["src"], mesh.shape["tgt"])


def local(mesh, n_src, n_tgt, comm=True):
    def per_device(xs, ys, a_mass, b_mass, s_region, t_region, allowed):
        width, n_i = xs.shape
        n_j = ys.shape[1]
        share = width // n_src
        tiles = n_i // TILE
        chips = n_tgt // 2
        piece = n_i // n_tgt
        vmem = pl.BlockSpec(memory_space=pltpu.VMEM)
        smem = pl.BlockSpec(memory_space=pltpu.SMEM)
        hbm = pl.BlockSpec(memory_space=pltpu.HBM)
        dma = pltpu.SemaphoreType.DMA

        def call(body, first, b_mass, s_region, t_region, f_shape, g_shape, scratch, identity):
            spare = (
                jax.ShapeDtypeStruct(g_shape, F32),
                jax.ShapeDtypeStruct((1,), jnp.int32),
                jax.ShapeDtypeStruct(s_region.shape, jnp.int32),
                jax.ShapeDtypeStruct(t_region.shape, jnp.int32),
            )
            return pl.pallas_call(
                functools.partial(body, n_src=n_src, n_tgt=n_tgt),
                out_shape=(
                    jax.ShapeDtypeStruct(f_shape, F32),
                    jax.ShapeDtypeStruct(g_shape, F32),
                    jax.ShapeDtypeStruct((share, n_j), F32),
                )
                + spare * first,
                in_specs=[hbm] * 7 if first else [vmem] * 4 + [smem] * 3,
                out_specs=(vmem, vmem, vmem) + (vmem, smem, smem, smem) * first,
                scratch_shapes=scratch,
                compiler_params=pltpu.CompilerParams(
                    collective_id=identity if comm else None,
                    has_side_effects=comm,
                    vmem_limit_bytes=VMEM_MIB * 1024 * 1024,
                ),
            )(xs, ys, a_mass.reshape(f_shape), b_mass.reshape(g_shape), s_region, t_region, allowed)

        f, g, projected, b_copy, failed, s_copy, t_copy = call(
            functools.partial(kernel, comm=comm), 1, b_mass, s_region, t_region, (n_i // LANES, LANES), (n_j // LANES, LANES),
            [
                pltpu.VMEM((width, n_j), BF16),
                pltpu.VMEM((n_i // LANES, LANES), F32),
                pltpu.VMEM((n_j // LANES, LANES), F32),
                pltpu.SMEM(s_region.shape, jnp.int32),
                pltpu.SMEM(t_region.shape, jnp.int32),
                pltpu.SMEM(allowed.shape, jnp.int32),
                pltpu.VMEM((256, n_i), BF16),
                pltpu.VMEM((256, n_j), BF16),
                pltpu.VMEM((n_j, 256), BF16),
                pltpu.VMEM((n_i, 128), BF16),
                pltpu.VMEM((n_j // LANES, LANES), F32),
                pltpu.VMEM((n_j, n_i), F32),
                pltpu.VMEM((n_j, LANES), F32),
                pltpu.VMEM((n_j, LANES), F32),
                pltpu.VMEM((n_i // LANES, LANES), F32),
                pltpu.VMEM((ITERS, tiles, 2, 8, LANES), F32),
                pltpu.VMEM((ITERS, tiles, chips, 8, LANES), F32),
                pltpu.VMEM((ITERS, n_src, 8, LANES), F32),
                pltpu.VMEM((n_j, LANES), F32),
                pltpu.VMEM((n_src, share, n_j), F32),
                pltpu.VMEM((n_src, share, n_j), F32),
                dma((9,)),
                dma((ITERS, tiles)), dma((ITERS, tiles)), dma((ITERS, tiles)), dma((ITERS, tiles)),
                dma((ITERS,)), dma((ITERS,)), dma, dma,
            ],
            0,
        )
        f, g = f.reshape(n_i), g.reshape(n_j)
        if not comm:
            return f, g, projected

        def careful():
            f, g, projected = call(
                careful_kernel, 0, b_copy, s_copy, t_copy, (1, n_i), (1, n_j),
                [
                    pltpu.VMEM((256, n_i), BF16),
                    pltpu.VMEM((256, n_j), BF16),
                    pltpu.VMEM((n_i, 256), BF16),
                    pltpu.VMEM((n_j, 256), BF16),
                    pltpu.VMEM((ITERS, 1, n_i), F32),
                    pltpu.VMEM((ITERS, 1, n_j), F32),
                    pltpu.VMEM((n_src, share, n_j), F32),
                    pltpu.VMEM((ITERS, n_tgt - 1, 1, piece), F32),
                    pltpu.VMEM((ITERS, 1, n_i), F32),
                    pltpu.VMEM((ITERS, n_src - 1, 1, n_j), F32),
                    pltpu.VMEM((n_src - 1, share, n_j), F32),
                    dma((ITERS,)), dma((ITERS,)), dma((ITERS,)), dma((ITERS,)),
                    dma((ITERS,)), dma((ITERS,)), dma, dma,
                ],
                1,
            )
            return f.reshape(n_i), g.reshape(n_j), projected

        return lax.cond(failed[0] > 0, careful, lambda: (f, g, projected))

    placed = (P(None, "src"), P(None, "tgt"), P("src"), P("tgt"), P("src"), P("tgt"), P())
    return jax.shard_map(
        per_device,
        mesh=mesh,
        in_specs=placed,
        out_specs=(P("src"), P("tgt"), P("src", "tgt")),
        check_vma=False,
    )
```

```python
import functools
import math

import jax
import jax.numpy as jnp
from jax import lax
from jax.experimental import pallas as pl
from jax.experimental.pallas import tpu as pltpu
from jax.sharding import PartitionSpec as P

SB = 1024
TB = 512
ITERS = 3
ENTROPIC = 0.05
MARGINAL = 1.0
DAMPING = MARGINAL / (MARGINAL + ENTROPIC)
KAPPA = math.log2(math.e) / ENTROPIC
FORBID = -(2.0**100)
MESH = pl.DeviceIdType.MESH
WIDE = 256
SUB = 256
ROWS = 32
LANES = 128
TILE = 1024
TAIL = 128
POT = TAIL + 32
VMEM_MIB = 63
SHIFT = 60.0
LARGEST = 2.0**110
F32 = jnp.float32
BF16 = jnp.bfloat16


def split3(value):
    high = value.astype(BF16).astype(F32)
    rest = value - high
    middle = rest.astype(BF16).astype(F32)
    return [high, middle, rest - middle]


def dot(a, b):
    return jnp.dot(a, b, preferred_element_type=F32)


def or_nan(safe, value):
    return jnp.where(safe, value, jnp.nan)


def put_potential(dense, into):
    stack = jnp.concatenate(split3(dense) + [jnp.zeros((8, LANES), F32)], axis=0)
    columns = stack.T
    lane = lax.broadcasted_iota(jnp.int32, columns.shape, 1)
    for block in range(8):
        own = jnp.where(lane % 8 == block, columns, 0.0)
        into[block * LANES : (block + 1) * LANES, TAIL : TAIL + 24] = own[:, :24].astype(BF16)


def lane_row(dense):
    return jnp.concatenate([dense[r : r + 1, :] for r in range(8)], axis=1)


def fold_lanes(values):
    return sum(values[:, at : at + LANES] for at in range(0, values.shape[1], LANES))


def farthest_first(n_src, n_tgt):
    hops = lambda d, n: min(d, n - d)
    chips = [(r // 4, r % 4) for r in range(1, n_tgt // 2)]
    chips.sort(key=lambda o: -(hops(o[0], n_tgt // 8) + hops(o[1], 4)))
    return sorted(range(1, n_src), key=lambda r: -hops(r, n_src)), chips


def kernel(
    xs_hbm, ys_hbm, a_hbm, b_hbm, s_hbm, t_hbm, allowed_hbm,
    f_out, g_out, projected, b_copy, failed, s_copy, t_copy,
    ys, a_mass, b_mass, s_region, t_region, allowed, x_aug, y_aug, y_t, x_t, y_term, coupling, w_col, acc, last_f,
    part_own, part_sib, pair_in, row_in, total_own, total_in, col_in, numer, numer_t, mass_in,
    load_sem, pair_sent, pair_recv, row_sent, row_recv, total_sent, total_recv, col_send, col_recv, mass_send, mass_recv,
    *, n_src, n_tgt, comm,
):
    width, n_j = ys.shape
    n_i = x_aug.shape[1]
    tiles = n_i // TILE
    half = tiles // 2
    chips = n_tgt // 2
    share = width // n_src
    src_order, chip_order = farthest_first(n_src, n_tgt)
    my_src = lax.axis_index("src")
    my_tgt = lax.axis_index("tgt")
    my_core = my_tgt % 2
    my_chip = my_tgt // 2
    sibling = (my_src, my_tgt + 1 - 2 * my_core)

    def chip_peer(offset):
        y = lax.rem(my_chip // 4 + offset[0], n_tgt // 8)
        return (my_src, (y * 4 + lax.rem(my_chip + offset[1], 4)) * 2 + my_core)

    def src_peer(offset):
        return (lax.rem(my_src + offset, n_src), my_tgt)

    loads = [
        pltpu.make_async_copy(source, target, load_sem.at[k])
        for k, (source, target) in enumerate((
            (ys_hbm, ys), (b_hbm, b_mass), (xs_hbm, x_aug.at[0:64]), (xs_hbm, x_aug.at[64:128]),
            (xs_hbm, x_aug.at[192:256]), (a_hbm, a_mass), (s_hbm, s_region), (t_hbm, t_region), (allowed_hbm, allowed),
        ))
    ]
    for load in loads:
        load.start()

    if comm:
        barrier = pltpu.get_barrier_semaphore()
        peers = [sibling] + [chip_peer(o) for o in chip_order] + [src_peer(o) for o in src_order]
        for peer in peers:
            pl.semaphore_signal(barrier, inc=1, device_id=peer, device_id_type=MESH)

    def send(src, dst, sent, received, peer):
        pltpu.make_async_remote_copy(
            src_ref=src, dst_ref=dst, send_sem=sent, recv_sem=received, device_id=peer, device_id_type=MESH
        ).start()

    def wait(ref, sem):
        pltpu.make_async_copy(ref, ref, sem).wait()

    row = lax.broadcasted_iota(jnp.int32, (32, n_i), 0)
    col = lax.broadcasted_iota(jnp.int32, (32, n_i), 1)
    x_aug[TAIL:POT, :] = jnp.where((row < 24) | (row - 24 == col // SB), 1.0, 0.0).astype(BF16)
    x_aug[POT + 16 : POT + 32, :] = jnp.zeros((16, n_i), BF16)
    for load in loads[:2] + loads[6:]:
        load.wait()
    row = lax.broadcasted_iota(jnp.int32, (8, n_j), 0)
    col = lax.broadcasted_iota(jnp.int32, (8, n_j), 1)
    mask = jnp.zeros((8, n_j), F32)
    for s in range(n_i // SB):
        for t in range(n_j // TB):
            keep = allowed[s_region[s], t_region[t]]
            here = (row == s) & (col // TB == t)
            mask = jnp.where(here, jnp.where(keep > 0, 0.0, FORBID), mask)
    ones = jnp.where(row < 3, 1.0, 0.0)
    tail = [jnp.zeros((24, n_j), F32), mask, ones, jnp.zeros((24, n_j), F32)]
    y_aug[TAIL : TAIL + 64, :] = jnp.concatenate(tail, axis=0).astype(BF16)
    y_wide = ys[...].astype(F32)
    y_parts = split3(y_wide * (2.0 * KAPPA / width))
    y_aug[0:64, :] = y_parts[0].astype(BF16)
    y_aug[64:128, :] = y_parts[1].astype(BF16)
    y_aug[192:256, :] = y_parts[2].astype(BF16)
    for c in range(n_j // WIDE):
        y_t[c * WIDE : (c + 1) * WIDE, :] = y_aug[:, c * WIDE : (c + 1) * WIDE].T
    y_squares = jnp.sum(y_wide * y_wide, axis=0, keepdims=True) * (-KAPPA / width)
    for c in range(n_j // LANES):
        y_term[c : c + 1, :] = y_squares[:, c * LANES : (c + 1) * LANES]
    b_log = jnp.log2(b_mass[...])
    put_potential(b_log + y_term[...] + SHIFT, y_t)
    for load in loads[2:6]:
        load.wait()
    row16 = lax.broadcasted_iota(jnp.int32, (16, TILE), 0)
    for s in range(tiles):
        at = slice(s * TILE, (s + 1) * TILE)
        x_wide = x_aug[0:64, at].astype(F32)
        x_term = jnp.sum(x_wide * x_wide, axis=0, keepdims=True) * (-KAPPA / width)
        tail = jnp.zeros((16, TILE), F32)
        for k, part in enumerate(split3(x_term)):
            tail = jnp.where(row16 == k, part, tail)
        x_aug[POT : POT + 16, at] = tail.astype(BF16)

    own_tiles = [my_core * half + q for q in range(half)]
    sib_tiles = [(1 - my_core) * half + q for q in range(half)]

    def tile_of(tile):
        return pl.ds(pl.multiple_of(tile * 8, 8), 8)

    def cells_of(tile):
        return pl.ds(pl.multiple_of(tile * TILE, TILE), TILE)

    def row_parts(it, sweep):
        for q, tile in enumerate(sib_tiles):
            sweep(tile, part_sib.at[it, q])
            if comm and it == 0 and q == 0:
                pl.semaphore_wait(barrier, len(peers))
            if comm:
                send(part_sib.at[it, q], pair_in.at[it, q], pair_sent.at[it, q], pair_recv.at[it, q], sibling)
        for q, tile in enumerate(own_tiles):
            sweep(tile, part_own.at[q])
            if comm:
                wait(pair_in.at[it, q], pair_recv.at[it, q])
            row_in[it, q, my_chip] = part_own[q] + pair_in[it, q]
            if comm:
                mine = row_in.at[it, q, my_chip]
                for offset in chip_order:
                    send(mine, mine, row_sent.at[it, q], row_recv.at[it, q], chip_peer(offset))

    def row_totals(it):
        for q, tile in enumerate(own_tiles):
            if comm:
                wait(row_in.at[it, q, pl.ds(0, chips - 1)], row_recv.at[it, q])
            total = jnp.sum(row_in[it, q], axis=0)
            total_own[it, q] = total
            if comm:
                send(total_own.at[it, q], total_in.at[it, q], total_sent.at[it, q], total_recv.at[it, q], sibling)
            yield q, tile, total
        for q, tile in enumerate(sib_tiles):
            if comm:
                wait(total_in.at[it, q], total_recv.at[it, q])
            yield half + q, tile, total_in[it, q]

    def source_factor(it, s, total):
        f2 = -DAMPING * (jnp.log2(total) - SHIFT)
        safe = (total >= 2.0 ** (SHIFT - 95.0)) & (total <= LARGEST)
        if it == ITERS - 1:
            safe &= jnp.abs(f2 - last_f[tile_of(s), :]) <= 8.0
        f2 = or_nan(safe, f2)
        last_f[tile_of(s), :] = f2
        return jnp.exp2(f2 + jnp.log2(a_mass[tile_of(s), :])), f2

    def target_total(it):
        for r in range(8):
            part = jnp.sum(acc[r * LANES : (r + 1) * LANES, :].T, axis=0, keepdims=True)
            col_in[it, my_src, r : r + 1, :] = part
        if comm:
            mine = col_in.at[it, my_src]
            for offset in src_order:
                send(mine, mine, col_send.at[it], col_recv.at[it], src_peer(offset))
            wait(col_in.at[it, pl.ds(0, n_src - 1)], col_recv.at[it])
        return jnp.sum(col_in[it], axis=0)

    def target_potential(total):
        return -DAMPING * (jnp.log2(total) - SHIFT - b_log)

    def target_factor(it):
        total = target_total(it)
        safe = (total >= 2.0 ** (SHIFT - 49.0)) & (total <= LARGEST)
        w = jnp.exp2(or_nan(safe, target_potential(total)))
        for r in range(8):
            w_col[r * LANES : (r + 1) * LANES, :] = jnp.broadcast_to(w[r : r + 1, :], (LANES, LANES)).T

    def first_row_sweep(tile, out):
        for c in range(TILE // WIDE):
            at = pl.ds(pl.multiple_of(tile * TILE + c * WIDE, WIDE), WIDE)
            rhs = x_aug[:, at]
            sums = jnp.zeros((8, WIDE), F32)
            for j in range(0, n_j, SUB):
                block = jnp.exp2(dot(y_t[j : j + SUB, :], rhs))
                coupling[j : j + SUB, at] = block
                sums += jnp.sum(block.reshape(SUB // 8, 8, WIDE), axis=0)
            value = jnp.sum(sums, axis=0, keepdims=True)
            for h in range(WIDE // LANES):
                r = c * (WIDE // LANES) + h
                out[r : r + 1, :] = value[:, h * LANES : (h + 1) * LANES]

    row_parts(0, first_row_sweep)
    for c in range(n_i // WIDE):
        x_t[c * WIDE : (c + 1) * WIDE, :] = x_aug[0:128, c * WIDE : (c + 1) * WIDE].T

    def row_sweep(tile, out):
        sums = jnp.zeros((8, TILE), F32)
        for j in range(0, n_j, ROWS):
            w = jnp.concatenate([w_col[j : j + ROWS, :]] * (TILE // LANES), axis=1)
            block = coupling[j : j + ROWS, cells_of(tile)] * w
            sums += jnp.sum(block.reshape(ROWS // 8, 8, TILE), axis=0)
        value = jnp.sum(sums, axis=0, keepdims=True)
        for r in range(8):
            out[r : r + 1, :] = value[:, r * LANES : (r + 1) * LANES]

    for it in range(ITERS - 1):
        if it > 0:
            row_parts(it, row_sweep)
        for place, tile, sums in row_totals(it):
            factor = lane_row(source_factor(it, tile, sums)[0])
            for j in range(0, n_j, ROWS):
                block = coupling[j : j + ROWS, cells_of(tile)] * factor
                part = fold_lanes(block)
                acc[j : j + ROWS, :] = part if place == 0 else acc[j : j + ROWS, :] + part
        target_factor(it)

    last = ITERS - 1
    row_parts(last, row_sweep)
    for place, tile, sums in row_totals(last):
        factor, f2 = source_factor(last, tile, sums)
        f_out[tile_of(tile), :] = f2 * (1.0 / KAPPA)
        factor = lane_row(factor)
        for j in range(0, n_j, SUB):
            rows = slice(j, j + SUB)
            weight = coupling[rows, cells_of(tile)] * factor
            part = fold_lanes(weight)
            product = dot(weight.astype(BF16), x_t[cells_of(tile), :])
            if place > 0:
                part += acc[rows, :]
                product += numer[rows, :]
            acc[rows, :] = part
            numer[rows, :] = product
            if place < tiles - 1:
                continue
            flat = product.T
            for d in range(n_src):
                numer_t[d, :, rows] = flat[d * share : (d + 1) * share, :]
            mass_in[my_src, :, rows] = numer_t[my_src, :, rows]
            if comm:
                for offset in src_order:
                    owner = lax.rem(my_src + offset, n_src)
                    send(
                        numer_t.at[owner, :, rows], mass_in.at[my_src, :, rows],
                        mass_send, mass_recv, (owner, my_tgt),
                    )
    total = target_total(last)
    g2 = target_potential(total)
    g_out[...] = g2 * (1.0 / KAPPA)
    for k in range(n_i // SB):
        s_copy[k] = s_region[k]
    for k in range(n_j // TB):
        t_copy[k] = t_region[k]
    b_copy[...] = b_mass[...]
    failed[0] = jnp.sum(jnp.where(g2 == g2, 0, 1))
    if comm:
        wait(mass_in.at[pl.ds(0, n_src - 1)], mass_recv)
    projected[...] = jnp.sum(mass_in[...], axis=0) / lane_row(total)

    if comm:
        for it in range(ITERS):
            for q in range(half):
                wait(pair_in.at[it, q], pair_sent.at[it, q])
                wait(row_in.at[it, q, pl.ds(0, chips - 1)], row_sent.at[it, q])
                wait(total_in.at[it, q], total_sent.at[it, q])
            wait(col_in.at[it, pl.ds(0, n_src - 1)], col_send.at[it])
        wait(mass_in.at[pl.ds(0, n_src - 1)], mass_send)


def tail_rows(at, parts, ones_at):
    shape = (16, parts[0].shape[1])
    row = lax.broadcasted_iota(jnp.int32, shape, 0)
    tail = jnp.where((row >= ones_at) & (row < ones_at + 3), 1.0, 0.0)
    for offset, part in enumerate(parts):
        tail = jnp.where(row == at + offset, jnp.broadcast_to(part, shape), tail)
    return tail


def careful_lse(scores):
    largest = jnp.max(scores, axis=0, keepdims=True)
    summed = jnp.sum(jnp.exp2(scores - largest), axis=0, keepdims=True)
    return largest + jnp.log2(summed)


def careful_kernel(
    xs, ys, a_mass, b_mass, s_region, t_region, allowed,
    f_out, g_out, projected,
    x_aug, y_aug, x_t, y_t, partial_row, partial_col, partial_mass,
    row_in, potential, col_in, mass_in,
    row_send, row_recv, pot_send, pot_recv, col_send, col_recv, mass_send, mass_recv,
    *, n_src, n_tgt,
):
    width, n_i = xs.shape
    n_j = ys.shape[1]
    my_src = lax.axis_index("src")
    my_tgt = lax.axis_index("tgt")
    piece = n_i // n_tgt
    share = width // n_src
    src_peer = lambda r: (lax.rem(my_src + r, n_src), my_tgt)
    tgt_peer = lambda r: (my_src, lax.rem(my_tgt + r, n_tgt))

    barrier = pltpu.get_barrier_semaphore()

    @pl.loop(1, n_tgt)
    def _(r):
        pl.semaphore_signal(barrier, inc=1, device_id=tgt_peer(r), device_id_type=MESH)

    @pl.loop(1, n_src)
    def _(r):
        pl.semaphore_signal(barrier, inc=1, device_id=src_peer(r), device_id_type=MESH)

    x = xs[...]
    x_wide = x.astype(F32)
    y_wide = ys[...].astype(F32)
    x_term = jnp.sum(x_wide * x_wide, axis=0, keepdims=True) * (-KAPPA / width)
    y_term = jnp.sum(y_wide * y_wide, axis=0, keepdims=True) * (-KAPPA / width)
    a_log = jnp.log2(a_mass[...])
    b_log = jnp.log2(b_mass[...])
    y_parts = split3(y_wide * (2.0 * KAPPA / width))

    x_aug[0:64, :] = x
    x_aug[64:128, :] = x
    x_aug[192:256, :] = x
    row16 = lax.broadcasted_iota(jnp.int32, (16, n_i), 0)
    col16 = lax.broadcasted_iota(jnp.int32, (16, n_i), 1)
    x_aug[128:144, :] = jnp.where((row16 >= 8) & (row16 < 11), 1.0, 0.0).astype(BF16)
    x_aug[144:160, :] = jnp.where(row16 == col16 // SB, 1.0, 0.0).astype(BF16)
    x_aug[160:192, :] = jnp.zeros((32, n_i), BF16)

    y_aug[0:64, :] = y_parts[0].astype(BF16)
    y_aug[64:128, :] = y_parts[1].astype(BF16)
    y_aug[192:256, :] = y_parts[2].astype(BF16)
    row16 = lax.broadcasted_iota(jnp.int32, (16, n_j), 0)
    col16 = lax.broadcasted_iota(jnp.int32, (16, n_j), 1)
    y_aug[128:144, :] = jnp.where(row16 < 3, 1.0, 0.0).astype(BF16)
    penalty = jnp.zeros((16, n_j), F32)
    for s in range(n_i // SB):
        for t in range(n_j // TB):
            keep = allowed[s_region[s], t_region[t]]
            here = (row16 == s) & (col16 // TB == t)
            penalty = jnp.where(here, jnp.where(keep > 0, 0.0, FORBID), penalty)
    y_aug[144:160, :] = penalty.astype(BF16)
    y_aug[160:192, :] = jnp.zeros((32, n_j), BF16)

    for c in range(n_i // WIDE):
        x_t[c * WIDE : (c + 1) * WIDE, :] = x_aug[:, c * WIDE : (c + 1) * WIDE].T
    for c in range(n_j // WIDE):
        y_t[c * WIDE : (c + 1) * WIDE, :] = y_aug[:, c * WIDE : (c + 1) * WIDE].T

    pl.semaphore_wait(barrier, n_tgt + n_src - 2)

    b_term = b_log + y_term
    col_lse = None
    for it in range(ITERS):
        score_b = b_term if it == 0 else b_term - DAMPING * (col_lse + y_term)
        y_t[:, 128:144] = tail_rows(8, split3(score_b), 0).T.astype(BF16)

        @pl.loop(0, n_i // WIDE)
        def _(c):
            at = pl.ds(pl.multiple_of(c * WIDE, WIDE), WIDE)
            partial_row[it, :, at] = careful_lse(jnp.dot(y_t[...], x_aug[:, at], preferred_element_type=F32))


        @pl.loop(1, n_tgt)
        def _(r):
            owner = lax.rem(my_tgt + r, n_tgt)
            pltpu.make_async_remote_copy(
                src_ref=partial_row.at[it, :, pl.ds(pl.multiple_of(owner * piece, piece), piece)],
                dst_ref=row_in.at[it, r - 1],
                send_sem=row_send.at[it],
                recv_sem=row_recv.at[it],
                device_id=(my_src, owner),
                device_id_type=MESH,
            ).start()

        mine = pl.ds(pl.multiple_of(my_tgt * piece, piece), piece)
        own = partial_row[it, :, mine]
        pltpu.make_async_copy(row_in.at[it], row_in.at[it], row_recv.at[it]).wait()
        others = row_in[it]
        largest = jnp.maximum(jnp.max(others, axis=0), own)
        summed = jnp.sum(jnp.exp2(others - largest[None]), axis=0) + jnp.exp2(own - largest)
        own = largest + jnp.log2(summed)
        potential[it, :, mine] = own

        @pl.loop(1, n_tgt)
        def _(r):
            pltpu.make_async_remote_copy(
                src_ref=potential.at[it, :, mine],
                dst_ref=potential.at[it, :, mine],
                send_sem=pot_send.at[it],
                recv_sem=pot_recv.at[it],
                device_id=tgt_peer(r),
                device_id_type=MESH,
            ).start()

        rest = potential.at[it, :, pl.ds(0, n_i - piece)]
        pltpu.make_async_copy(rest, rest, pot_recv.at[it]).wait()

        f2 = -DAMPING * (potential[it] + x_term)
        if it == ITERS - 1:
            f_out[...] = f2 * (1.0 / KAPPA)
        score_a = a_log + f2 + x_term
        x_t[:, 128:144] = tail_rows(0, split3(score_a), 8).T.astype(BF16)

        @pl.loop(0, n_j // WIDE)
        def _(c):
            at = pl.ds(pl.multiple_of(c * WIDE, WIDE), WIDE)
            rhs = y_aug[:, at]
            parts = [
                careful_lse(jnp.dot(x_t[s * SB : (s + 1) * SB, :], rhs, preferred_element_type=F32))
                for s in range(n_i // SB)
            ]
            largest = functools.reduce(jnp.maximum, parts)
            summed = sum(jnp.exp2(part - largest) for part in parts)
            partial_col[it, :, at] = largest + jnp.log2(summed)

        col_lse = partial_col[it]

        @pl.loop(1, n_src)
        def _(r):
            pltpu.make_async_remote_copy(
                src_ref=partial_col.at[it],
                dst_ref=col_in.at[it, r - 1],
                send_sem=col_send.at[it],
                recv_sem=col_recv.at[it],
                device_id=src_peer(r),
                device_id_type=MESH,
            ).start()

        pltpu.make_async_copy(col_in.at[it], col_in.at[it], col_recv.at[it]).wait()
        others = col_in[it]
        largest = jnp.maximum(jnp.max(others, axis=0), col_lse)
        summed = jnp.sum(jnp.exp2(others - largest[None]), axis=0) + jnp.exp2(col_lse - largest)
        col_lse = largest + jnp.log2(summed)

    g_out[...] = (-DAMPING / KAPPA) * (col_lse + y_term)

    y_aug[128:144, :] = tail_rows(8, split3(-col_lse), 0).astype(BF16)

    @pl.loop(0, n_j // WIDE)
    def _(c):
        at = pl.ds(pl.multiple_of(c * WIDE, WIDE), WIDE)
        rhs = y_aug[:, at]
        total = jnp.zeros((width, WIDE), F32)
        for s in range(n_i // SB):
            scores = jnp.dot(x_t[s * SB : (s + 1) * SB, :], rhs, preferred_element_type=F32)
            weight = jnp.exp2(scores).astype(BF16)
            total += jnp.dot(xs[:, s * SB : (s + 1) * SB], weight, preferred_element_type=F32)
        for k in range(n_src):
            partial_mass[k, :, at] = total[k * share : (k + 1) * share]

    result = partial_mass[my_src]

    @pl.loop(1, n_src)
    def _(r):
        owner = lax.rem(my_src + r, n_src)
        pltpu.make_async_remote_copy(
            src_ref=partial_mass.at[owner],
            dst_ref=mass_in.at[r - 1],
            send_sem=mass_send,
            recv_sem=mass_recv,
            device_id=(owner, my_tgt),
            device_id_type=MESH,
        ).start()

    pltpu.make_async_copy(mass_in, mass_in, mass_recv).wait()
    result = result + jnp.sum(mass_in[...], axis=0)
    projected[...] = result

    for it in range(ITERS):
        pltpu.make_async_copy(row_in.at[it], row_in.at[it], row_send.at[it]).wait()
        rest = potential.at[it, :, pl.ds(0, n_i - piece)]
        pltpu.make_async_copy(rest, rest, pot_send.at[it]).wait()
        pltpu.make_async_copy(col_in.at[it], col_in.at[it], col_send.at[it]).wait()
    pltpu.make_async_copy(mass_in, mass_in, mass_send).wait()


def solution(mesh):
    return local(mesh, mesh.shape["src"], mesh.shape["tgt"])


def local(mesh, n_src, n_tgt, comm=True):
    def per_device(xs, ys, a_mass, b_mass, s_region, t_region, allowed):
        width, n_i = xs.shape
        n_j = ys.shape[1]
        share = width // n_src
        tiles = n_i // TILE
        half = tiles // 2
        chips = n_tgt // 2
        piece = n_i // n_tgt
        vmem = pl.BlockSpec(memory_space=pltpu.VMEM)
        smem = pl.BlockSpec(memory_space=pltpu.SMEM)
        hbm = pl.BlockSpec(memory_space=pltpu.HBM)
        dma = pltpu.SemaphoreType.DMA

        def call(body, first, b_mass, s_region, t_region, f_shape, g_shape, scratch, identity):
            spare = (
                jax.ShapeDtypeStruct(g_shape, F32),
                jax.ShapeDtypeStruct((1,), jnp.int32),
                jax.ShapeDtypeStruct(s_region.shape, jnp.int32),
                jax.ShapeDtypeStruct(t_region.shape, jnp.int32),
            )
            return pl.pallas_call(
                functools.partial(body, n_src=n_src, n_tgt=n_tgt),
                out_shape=(
                    jax.ShapeDtypeStruct(f_shape, F32),
                    jax.ShapeDtypeStruct(g_shape, F32),
                    jax.ShapeDtypeStruct((share, n_j), F32),
                )
                + spare * first,
                in_specs=[hbm] * 7 if first else [vmem] * 4 + [smem] * 3,
                out_specs=(vmem, vmem, vmem) + (vmem, smem, smem, smem) * first,
                scratch_shapes=scratch,
                compiler_params=pltpu.CompilerParams(
                    collective_id=identity if comm else None,
                    has_side_effects=comm,
                    vmem_limit_bytes=VMEM_MIB * 1024 * 1024,
                ),
            )(xs, ys, a_mass.reshape(f_shape), b_mass.reshape(g_shape), s_region, t_region, allowed)

        f, g, projected, b_copy, failed, s_copy, t_copy = call(
            functools.partial(kernel, comm=comm), 1, b_mass, s_region, t_region, (n_i // LANES, LANES), (n_j // LANES, LANES),
            [
                pltpu.VMEM((width, n_j), BF16),
                pltpu.VMEM((n_i // LANES, LANES), F32),
                pltpu.VMEM((n_j // LANES, LANES), F32),
                pltpu.SMEM(s_region.shape, jnp.int32),
                pltpu.SMEM(t_region.shape, jnp.int32),
                pltpu.SMEM(allowed.shape, jnp.int32),
                pltpu.VMEM((256, n_i), BF16),
                pltpu.VMEM((256, n_j), BF16),
                pltpu.VMEM((n_j, 256), BF16),
                pltpu.VMEM((n_i, 128), BF16),
                pltpu.VMEM((n_j // LANES, LANES), F32),
                pltpu.VMEM((n_j, n_i), F32),
                pltpu.VMEM((n_j, LANES), F32),
                pltpu.VMEM((n_j, LANES), F32),
                pltpu.VMEM((n_i // LANES, LANES), F32),
                pltpu.VMEM((half, 8, LANES), F32),
                pltpu.VMEM((ITERS, half, 8, LANES), F32),
                pltpu.VMEM((ITERS, half, 8, LANES), F32),
                pltpu.VMEM((ITERS, half, chips, 8, LANES), F32),
                pltpu.VMEM((ITERS, half, 8, LANES), F32),
                pltpu.VMEM((ITERS, half, 8, LANES), F32),
                pltpu.VMEM((ITERS, n_src, 8, LANES), F32),
                pltpu.VMEM((n_j, LANES), F32),
                pltpu.VMEM((n_src, share, n_j), F32),
                pltpu.VMEM((n_src, share, n_j), F32),
                dma((9,)),
                *[dma((ITERS, half))] * 6,
                dma((ITERS,)), dma((ITERS,)), dma, dma,
            ],
            0,
        )
        f, g = f.reshape(n_i), g.reshape(n_j)
        if not comm:
            return f, g, projected

        def careful():
            f, g, projected = call(
                careful_kernel, 0, b_copy, s_copy, t_copy, (1, n_i), (1, n_j),
                [
                    pltpu.VMEM((256, n_i), BF16),
                    pltpu.VMEM((256, n_j), BF16),
                    pltpu.VMEM((n_i, 256), BF16),
                    pltpu.VMEM((n_j, 256), BF16),
                    pltpu.VMEM((ITERS, 1, n_i), F32),
                    pltpu.VMEM((ITERS, 1, n_j), F32),
                    pltpu.VMEM((n_src, share, n_j), F32),
                    pltpu.VMEM((ITERS, n_tgt - 1, 1, piece), F32),
                    pltpu.VMEM((ITERS, 1, n_i), F32),
                    pltpu.VMEM((ITERS, n_src - 1, 1, n_j), F32),
                    pltpu.VMEM((n_src - 1, share, n_j), F32),
                    dma((ITERS,)), dma((ITERS,)), dma((ITERS,)), dma((ITERS,)),
                    dma((ITERS,)), dma((ITERS,)), dma, dma,
                ],
                1,
            )
            return f.reshape(n_i), g.reshape(n_j), projected

        return lax.cond(failed[0] > 0, careful, lambda: (f, g, projected))

    placed = (P(None, "src"), P(None, "tgt"), P("src"), P("tgt"), P("src"), P("tgt"), P())
    return jax.shard_map(
        per_device,
        mesh=mesh,
        in_specs=placed,
        out_specs=(P("src"), P("tgt"), P("src", "tgt")),
        check_vma=False,
    )
```

```python
import functools
import math

import jax
import jax.numpy as jnp
from jax import lax
from jax.experimental import pallas as pl
from jax.experimental.pallas import tpu as pltpu
from jax.sharding import PartitionSpec as P

SB = 1024
TB = 512
ITERS = 3
ENTROPIC = 0.05
MARGINAL = 1.0
DAMPING = MARGINAL / (MARGINAL + ENTROPIC)
KAPPA = math.log2(math.e) / ENTROPIC
FORBID = -(2.0**100)
MESH = pl.DeviceIdType.MESH
WIDE = 256
SUB = 512
ROWS = 32
LANES = 128
TILE = 1024
TAIL = 128
POT = TAIL + 32
VMEM_MIB = 63
SHIFT = 60.0
LARGEST = 2.0**110
F32 = jnp.float32
BF16 = jnp.bfloat16


def split3(value):
    high = value.astype(BF16).astype(F32)
    rest = value - high
    middle = rest.astype(BF16).astype(F32)
    return [high, middle, rest - middle]


def dot(a, b):
    return jnp.dot(a, b, preferred_element_type=F32)


def or_nan(safe, value):
    return jnp.where(safe, value, jnp.nan)


def put_potential(dense, into):
    stack = jnp.concatenate(split3(dense) + [jnp.zeros((8, LANES), F32)], axis=0)
    columns = stack.T
    lane = lax.broadcasted_iota(jnp.int32, columns.shape, 1)
    for block in range(8):
        own = jnp.where(lane % 8 == block, columns, 0.0)
        into[block * LANES : (block + 1) * LANES, TAIL : TAIL + 24] = own[:, :24].astype(BF16)


def lane_row(dense):
    return jnp.concatenate([dense[r : r + 1, :] for r in range(8)], axis=1)


def fold_lanes(values):
    return sum(values[:, at : at + LANES] for at in range(0, values.shape[1], LANES))


def farthest_first(n_src, n_tgt):
    hops = lambda d, n: min(d, n - d)
    chips = [(r // 4, r % 4) for r in range(1, n_tgt // 2)]
    chips.sort(key=lambda o: -(hops(o[0], n_tgt // 8) + hops(o[1], 4)))
    return sorted(range(1, n_src), key=lambda r: -hops(r, n_src)), chips


def kernel(
    xs_hbm, ys_hbm, a_hbm, b_hbm, s_hbm, t_hbm, allowed_hbm,
    f_out, g_out, projected, b_copy, failed, s_copy, t_copy,
    ys, a_mass, b_mass, s_region, t_region, allowed, x_aug, y_aug, y_t, x_t, y_term, coupling, w_col, acc, last_f,
    part_own, part_sib, pair_in, row_in, total_own, total_in, col_in, numer, numer_t, mass_in,
    load_sem, pair_sent, pair_recv, row_sent, row_recv, total_sent, total_recv, col_send, col_recv, mass_send, mass_recv,
    *, n_src, n_tgt, comm,
):
    width, n_j = ys.shape
    n_i = x_aug.shape[1]
    tiles = n_i // TILE
    half = tiles // 2
    chips = n_tgt // 2
    share = width // n_src
    src_order, chip_order = farthest_first(n_src, n_tgt)
    my_src = lax.axis_index("src")
    my_tgt = lax.axis_index("tgt")
    my_core = my_tgt % 2
    my_chip = my_tgt // 2
    sibling = (my_src, my_tgt + 1 - 2 * my_core)

    def chip_peer(offset):
        y = lax.rem(my_chip // 4 + offset[0], n_tgt // 8)
        return (my_src, (y * 4 + lax.rem(my_chip + offset[1], 4)) * 2 + my_core)

    def src_peer(offset):
        return (lax.rem(my_src + offset, n_src), my_tgt)

    loads = [
        pltpu.make_async_copy(source, target, load_sem.at[k])
        for k, (source, target) in enumerate((
            (ys_hbm, ys), (b_hbm, b_mass), (xs_hbm, x_aug.at[0:64]), (xs_hbm, x_aug.at[64:128]),
            (xs_hbm, x_aug.at[192:256]), (a_hbm, a_mass), (s_hbm, s_region), (t_hbm, t_region), (allowed_hbm, allowed),
        ))
    ]
    for load in loads:
        load.start()

    if comm:
        barrier = pltpu.get_barrier_semaphore()
        peers = [sibling] + [chip_peer(o) for o in chip_order] + [src_peer(o) for o in src_order]
        for peer in peers:
            pl.semaphore_signal(barrier, inc=1, device_id=peer, device_id_type=MESH)

    def send(src, dst, sent, received, peer):
        pltpu.make_async_remote_copy(
            src_ref=src, dst_ref=dst, send_sem=sent, recv_sem=received, device_id=peer, device_id_type=MESH
        ).start()

    def wait(ref, sem):
        pltpu.make_async_copy(ref, ref, sem).wait()

    row = lax.broadcasted_iota(jnp.int32, (32, n_i), 0)
    col = lax.broadcasted_iota(jnp.int32, (32, n_i), 1)
    x_aug[TAIL:POT, :] = jnp.where((row < 24) | (row - 24 == col // SB), 1.0, 0.0).astype(BF16)
    x_aug[POT + 16 : POT + 32, :] = jnp.zeros((16, n_i), BF16)
    for load in loads[:2] + loads[6:]:
        load.wait()
    row = lax.broadcasted_iota(jnp.int32, (8, n_j), 0)
    col = lax.broadcasted_iota(jnp.int32, (8, n_j), 1)
    mask = jnp.zeros((8, n_j), F32)
    for s in range(n_i // SB):
        for t in range(n_j // TB):
            keep = allowed[s_region[s], t_region[t]]
            here = (row == s) & (col // TB == t)
            mask = jnp.where(here, jnp.where(keep > 0, 0.0, FORBID), mask)
    ones = jnp.where(row < 3, 1.0, 0.0)
    tail = [jnp.zeros((24, n_j), F32), mask, ones, jnp.zeros((24, n_j), F32)]
    y_aug[TAIL : TAIL + 64, :] = jnp.concatenate(tail, axis=0).astype(BF16)
    y_wide = ys[...].astype(F32)
    y_parts = split3(y_wide * (2.0 * KAPPA / width))
    y_aug[0:64, :] = y_parts[0].astype(BF16)
    y_aug[64:128, :] = y_parts[1].astype(BF16)
    y_aug[192:256, :] = y_parts[2].astype(BF16)
    for c in range(n_j // WIDE):
        y_t[c * WIDE : (c + 1) * WIDE, :] = y_aug[:, c * WIDE : (c + 1) * WIDE].T
    y_squares = jnp.sum(y_wide * y_wide, axis=0, keepdims=True) * (-KAPPA / width)
    for c in range(n_j // LANES):
        y_term[c : c + 1, :] = y_squares[:, c * LANES : (c + 1) * LANES]
    b_log = jnp.log2(b_mass[...])
    put_potential(b_log + y_term[...] + SHIFT, y_t)
    for load in loads[2:6]:
        load.wait()
    row16 = lax.broadcasted_iota(jnp.int32, (16, TILE), 0)
    for s in range(tiles):
        at = slice(s * TILE, (s + 1) * TILE)
        x_wide = x_aug[0:64, at].astype(F32)
        x_term = jnp.sum(x_wide * x_wide, axis=0, keepdims=True) * (-KAPPA / width)
        tail = jnp.zeros((16, TILE), F32)
        for k, part in enumerate(split3(x_term)):
            tail = jnp.where(row16 == k, part, tail)
        x_aug[POT : POT + 16, at] = tail.astype(BF16)

    own_tiles = [my_core * half + q for q in range(half)]
    sib_tiles = [(1 - my_core) * half + q for q in range(half)]

    def tile_of(tile):
        return pl.ds(pl.multiple_of(tile * 8, 8), 8)

    def cells_of(tile):
        return pl.ds(pl.multiple_of(tile * TILE, TILE), TILE)

    def row_parts(it, sweep):
        for q, tile in enumerate(sib_tiles):
            sweep(tile, part_sib.at[it, q])
            if comm and it == 0 and q == 0:
                pl.semaphore_wait(barrier, len(peers))
            if comm:
                send(part_sib.at[it, q], pair_in.at[it, q], pair_sent.at[it, q], pair_recv.at[it, q], sibling)
        for q, tile in enumerate(own_tiles):
            sweep(tile, part_own.at[q])
            if comm:
                wait(pair_in.at[it, q], pair_recv.at[it, q])
            row_in[it, q, my_chip] = part_own[q] + pair_in[it, q]
            if comm:
                mine = row_in.at[it, q, my_chip]
                for offset in chip_order:
                    send(mine, mine, row_sent.at[it, q], row_recv.at[it, q], chip_peer(offset))

    def row_totals(it):
        for q, tile in enumerate(own_tiles):
            if comm:
                wait(row_in.at[it, q, pl.ds(0, chips - 1)], row_recv.at[it, q])
            total = jnp.sum(row_in[it, q], axis=0)
            total_own[it, q] = total
            if comm:
                send(total_own.at[it, q], total_in.at[it, q], total_sent.at[it, q], total_recv.at[it, q], sibling)
            yield q, tile, total
        for q, tile in enumerate(sib_tiles):
            if comm:
                wait(total_in.at[it, q], total_recv.at[it, q])
            yield half + q, tile, total_in[it, q]

    def source_factor(it, s, total):
        f2 = -DAMPING * (jnp.log2(total) - SHIFT)
        safe = (total >= 2.0 ** (SHIFT - 95.0)) & (total <= LARGEST)
        if it == ITERS - 1:
            safe &= jnp.abs(f2 - last_f[tile_of(s), :]) <= 8.0
        f2 = or_nan(safe, f2)
        last_f[tile_of(s), :] = f2
        return jnp.exp2(f2 + jnp.log2(a_mass[tile_of(s), :])), f2

    def target_total(it):
        for r in range(8):
            part = jnp.sum(acc[r * LANES : (r + 1) * LANES, :].T, axis=0, keepdims=True)
            col_in[it, my_src, r : r + 1, :] = part
        if comm:
            mine = col_in.at[it, my_src]
            for offset in src_order:
                send(mine, mine, col_send.at[it], col_recv.at[it], src_peer(offset))
            wait(col_in.at[it, pl.ds(0, n_src - 1)], col_recv.at[it])
        return jnp.sum(col_in[it], axis=0)

    def target_potential(total):
        return -DAMPING * (jnp.log2(total) - SHIFT - b_log)

    def target_factor(it):
        total = target_total(it)
        safe = (total >= 2.0 ** (SHIFT - 49.0)) & (total <= LARGEST)
        w = jnp.exp2(or_nan(safe, target_potential(total)))
        for r in range(8):
            w_col[r * LANES : (r + 1) * LANES, :] = jnp.broadcast_to(w[r : r + 1, :], (LANES, LANES)).T

    def first_row_sweep(tile, out):
        for c in range(TILE // WIDE):
            at = pl.ds(pl.multiple_of(tile * TILE + c * WIDE, WIDE), WIDE)
            rhs = x_aug[:, at]
            sums = jnp.zeros((8, WIDE), F32)
            for j in range(0, n_j, SUB):
                block = jnp.exp2(dot(y_t[j : j + SUB, :], rhs))
                coupling[j : j + SUB, at] = block
                sums += jnp.sum(block.reshape(SUB // 8, 8, WIDE), axis=0)
            value = jnp.sum(sums, axis=0, keepdims=True)
            for h in range(WIDE // LANES):
                r = c * (WIDE // LANES) + h
                out[r : r + 1, :] = value[:, h * LANES : (h + 1) * LANES]

    row_parts(0, first_row_sweep)
    for c in range(n_i // WIDE):
        x_t[c * WIDE : (c + 1) * WIDE, :] = x_aug[0:128, c * WIDE : (c + 1) * WIDE].T

    def row_sweep(tile, out):
        sums = jnp.zeros((8, TILE), F32)
        for j in range(0, n_j, ROWS):
            w = jnp.concatenate([w_col[j : j + ROWS, :]] * (TILE // LANES), axis=1)
            block = coupling[j : j + ROWS, cells_of(tile)] * w
            sums += jnp.sum(block.reshape(ROWS // 8, 8, TILE), axis=0)
        value = jnp.sum(sums, axis=0, keepdims=True)
        for r in range(8):
            out[r : r + 1, :] = value[:, r * LANES : (r + 1) * LANES]

    for it in range(ITERS - 1):
        if it > 0:
            row_parts(it, row_sweep)
        for place, tile, sums in row_totals(it):
            factor = lane_row(source_factor(it, tile, sums)[0])
            for j in range(0, n_j, ROWS):
                block = coupling[j : j + ROWS, cells_of(tile)] * factor
                part = fold_lanes(block)
                acc[j : j + ROWS, :] = part if place == 0 else acc[j : j + ROWS, :] + part
        target_factor(it)

    last = ITERS - 1
    row_parts(last, row_sweep)
    for place, tile, sums in row_totals(last):
        factor, f2 = source_factor(last, tile, sums)
        f_out[tile_of(tile), :] = f2 * (1.0 / KAPPA)
        factor = lane_row(factor)
        for j in range(0, n_j, SUB):
            rows = slice(j, j + SUB)
            weight = coupling[rows, cells_of(tile)] * factor
            part = fold_lanes(weight)
            product = dot(weight.astype(BF16), x_t[cells_of(tile), :])
            if place > 0:
                part += acc[rows, :]
                product += numer[rows, :]
            acc[rows, :] = part
            numer[rows, :] = product
            if place < tiles - 1:
                continue
            flat = product.T
            for d in range(n_src):
                numer_t[d, :, rows] = flat[d * share : (d + 1) * share, :]
            mass_in[my_src, :, rows] = numer_t[my_src, :, rows]
            if comm:
                for offset in src_order:
                    owner = lax.rem(my_src + offset, n_src)
                    send(
                        numer_t.at[owner, :, rows], mass_in.at[my_src, :, rows],
                        mass_send, mass_recv, (owner, my_tgt),
                    )
    total = target_total(last)
    g2 = target_potential(total)
    g_out[...] = g2 * (1.0 / KAPPA)
    for k in range(n_i // SB):
        s_copy[k] = s_region[k]
    for k in range(n_j // TB):
        t_copy[k] = t_region[k]
    b_copy[...] = b_mass[...]
    failed[0] = jnp.sum(jnp.where(g2 == g2, 0, 1))
    if comm:
        wait(mass_in.at[pl.ds(0, n_src - 1)], mass_recv)
    projected[...] = jnp.sum(mass_in[...], axis=0) / lane_row(total)

    if comm:
        for it in range(ITERS):
            for q in range(half):
                wait(pair_in.at[it, q], pair_sent.at[it, q])
                wait(row_in.at[it, q, pl.ds(0, chips - 1)], row_sent.at[it, q])
                wait(total_in.at[it, q], total_sent.at[it, q])
            wait(col_in.at[it, pl.ds(0, n_src - 1)], col_send.at[it])
        wait(mass_in.at[pl.ds(0, n_src - 1)], mass_send)


def tail_rows(at, parts, ones_at):
    shape = (16, parts[0].shape[1])
    row = lax.broadcasted_iota(jnp.int32, shape, 0)
    tail = jnp.where((row >= ones_at) & (row < ones_at + 3), 1.0, 0.0)
    for offset, part in enumerate(parts):
        tail = jnp.where(row == at + offset, jnp.broadcast_to(part, shape), tail)
    return tail


def careful_lse(scores):
    largest = jnp.max(scores, axis=0, keepdims=True)
    summed = jnp.sum(jnp.exp2(scores - largest), axis=0, keepdims=True)
    return largest + jnp.log2(summed)


def careful_kernel(
    xs, ys, a_mass, b_mass, s_region, t_region, allowed,
    f_out, g_out, projected,
    x_aug, y_aug, x_t, y_t, partial_row, partial_col, partial_mass,
    row_in, potential, col_in, mass_in,
    row_send, row_recv, pot_send, pot_recv, col_send, col_recv, mass_send, mass_recv,
    *, n_src, n_tgt,
):
    width, n_i = xs.shape
    n_j = ys.shape[1]
    my_src = lax.axis_index("src")
    my_tgt = lax.axis_index("tgt")
    piece = n_i // n_tgt
    share = width // n_src
    src_peer = lambda r: (lax.rem(my_src + r, n_src), my_tgt)
    tgt_peer = lambda r: (my_src, lax.rem(my_tgt + r, n_tgt))

    barrier = pltpu.get_barrier_semaphore()

    @pl.loop(1, n_tgt)
    def _(r):
        pl.semaphore_signal(barrier, inc=1, device_id=tgt_peer(r), device_id_type=MESH)

    @pl.loop(1, n_src)
    def _(r):
        pl.semaphore_signal(barrier, inc=1, device_id=src_peer(r), device_id_type=MESH)

    x = xs[...]
    x_wide = x.astype(F32)
    y_wide = ys[...].astype(F32)
    x_term = jnp.sum(x_wide * x_wide, axis=0, keepdims=True) * (-KAPPA / width)
    y_term = jnp.sum(y_wide * y_wide, axis=0, keepdims=True) * (-KAPPA / width)
    a_log = jnp.log2(a_mass[...])
    b_log = jnp.log2(b_mass[...])
    y_parts = split3(y_wide * (2.0 * KAPPA / width))

    x_aug[0:64, :] = x
    x_aug[64:128, :] = x
    x_aug[192:256, :] = x
    row16 = lax.broadcasted_iota(jnp.int32, (16, n_i), 0)
    col16 = lax.broadcasted_iota(jnp.int32, (16, n_i), 1)
    x_aug[128:144, :] = jnp.where((row16 >= 8) & (row16 < 11), 1.0, 0.0).astype(BF16)
    x_aug[144:160, :] = jnp.where(row16 == col16 // SB, 1.0, 0.0).astype(BF16)
    x_aug[160:192, :] = jnp.zeros((32, n_i), BF16)

    y_aug[0:64, :] = y_parts[0].astype(BF16)
    y_aug[64:128, :] = y_parts[1].astype(BF16)
    y_aug[192:256, :] = y_parts[2].astype(BF16)
    row16 = lax.broadcasted_iota(jnp.int32, (16, n_j), 0)
    col16 = lax.broadcasted_iota(jnp.int32, (16, n_j), 1)
    y_aug[128:144, :] = jnp.where(row16 < 3, 1.0, 0.0).astype(BF16)
    penalty = jnp.zeros((16, n_j), F32)
    for s in range(n_i // SB):
        for t in range(n_j // TB):
            keep = allowed[s_region[s], t_region[t]]
            here = (row16 == s) & (col16 // TB == t)
            penalty = jnp.where(here, jnp.where(keep > 0, 0.0, FORBID), penalty)
    y_aug[144:160, :] = penalty.astype(BF16)
    y_aug[160:192, :] = jnp.zeros((32, n_j), BF16)

    for c in range(n_i // WIDE):
        x_t[c * WIDE : (c + 1) * WIDE, :] = x_aug[:, c * WIDE : (c + 1) * WIDE].T
    for c in range(n_j // WIDE):
        y_t[c * WIDE : (c + 1) * WIDE, :] = y_aug[:, c * WIDE : (c + 1) * WIDE].T

    pl.semaphore_wait(barrier, n_tgt + n_src - 2)

    b_term = b_log + y_term
    col_lse = None
    for it in range(ITERS):
        score_b = b_term if it == 0 else b_term - DAMPING * (col_lse + y_term)
        y_t[:, 128:144] = tail_rows(8, split3(score_b), 0).T.astype(BF16)

        @pl.loop(0, n_i // WIDE)
        def _(c):
            at = pl.ds(pl.multiple_of(c * WIDE, WIDE), WIDE)
            partial_row[it, :, at] = careful_lse(jnp.dot(y_t[...], x_aug[:, at], preferred_element_type=F32))


        @pl.loop(1, n_tgt)
        def _(r):
            owner = lax.rem(my_tgt + r, n_tgt)
            pltpu.make_async_remote_copy(
                src_ref=partial_row.at[it, :, pl.ds(pl.multiple_of(owner * piece, piece), piece)],
                dst_ref=row_in.at[it, r - 1],
                send_sem=row_send.at[it],
                recv_sem=row_recv.at[it],
                device_id=(my_src, owner),
                device_id_type=MESH,
            ).start()

        mine = pl.ds(pl.multiple_of(my_tgt * piece, piece), piece)
        own = partial_row[it, :, mine]
        pltpu.make_async_copy(row_in.at[it], row_in.at[it], row_recv.at[it]).wait()
        others = row_in[it]
        largest = jnp.maximum(jnp.max(others, axis=0), own)
        summed = jnp.sum(jnp.exp2(others - largest[None]), axis=0) + jnp.exp2(own - largest)
        own = largest + jnp.log2(summed)
        potential[it, :, mine] = own

        @pl.loop(1, n_tgt)
        def _(r):
            pltpu.make_async_remote_copy(
                src_ref=potential.at[it, :, mine],
                dst_ref=potential.at[it, :, mine],
                send_sem=pot_send.at[it],
                recv_sem=pot_recv.at[it],
                device_id=tgt_peer(r),
                device_id_type=MESH,
            ).start()

        rest = potential.at[it, :, pl.ds(0, n_i - piece)]
        pltpu.make_async_copy(rest, rest, pot_recv.at[it]).wait()

        f2 = -DAMPING * (potential[it] + x_term)
        if it == ITERS - 1:
            f_out[...] = f2 * (1.0 / KAPPA)
        score_a = a_log + f2 + x_term
        x_t[:, 128:144] = tail_rows(0, split3(score_a), 8).T.astype(BF16)

        @pl.loop(0, n_j // WIDE)
        def _(c):
            at = pl.ds(pl.multiple_of(c * WIDE, WIDE), WIDE)
            rhs = y_aug[:, at]
            parts = [
                careful_lse(jnp.dot(x_t[s * SB : (s + 1) * SB, :], rhs, preferred_element_type=F32))
                for s in range(n_i // SB)
            ]
            largest = functools.reduce(jnp.maximum, parts)
            summed = sum(jnp.exp2(part - largest) for part in parts)
            partial_col[it, :, at] = largest + jnp.log2(summed)

        col_lse = partial_col[it]

        @pl.loop(1, n_src)
        def _(r):
            pltpu.make_async_remote_copy(
                src_ref=partial_col.at[it],
                dst_ref=col_in.at[it, r - 1],
                send_sem=col_send.at[it],
                recv_sem=col_recv.at[it],
                device_id=src_peer(r),
                device_id_type=MESH,
            ).start()

        pltpu.make_async_copy(col_in.at[it], col_in.at[it], col_recv.at[it]).wait()
        others = col_in[it]
        largest = jnp.maximum(jnp.max(others, axis=0), col_lse)
        summed = jnp.sum(jnp.exp2(others - largest[None]), axis=0) + jnp.exp2(col_lse - largest)
        col_lse = largest + jnp.log2(summed)

    g_out[...] = (-DAMPING / KAPPA) * (col_lse + y_term)

    y_aug[128:144, :] = tail_rows(8, split3(-col_lse), 0).astype(BF16)

    @pl.loop(0, n_j // WIDE)
    def _(c):
        at = pl.ds(pl.multiple_of(c * WIDE, WIDE), WIDE)
        rhs = y_aug[:, at]
        total = jnp.zeros((width, WIDE), F32)
        for s in range(n_i // SB):
            scores = jnp.dot(x_t[s * SB : (s + 1) * SB, :], rhs, preferred_element_type=F32)
            weight = jnp.exp2(scores).astype(BF16)
            total += jnp.dot(xs[:, s * SB : (s + 1) * SB], weight, preferred_element_type=F32)
        for k in range(n_src):
            partial_mass[k, :, at] = total[k * share : (k + 1) * share]

    result = partial_mass[my_src]

    @pl.loop(1, n_src)
    def _(r):
        owner = lax.rem(my_src + r, n_src)
        pltpu.make_async_remote_copy(
            src_ref=partial_mass.at[owner],
            dst_ref=mass_in.at[r - 1],
            send_sem=mass_send,
            recv_sem=mass_recv,
            device_id=(owner, my_tgt),
            device_id_type=MESH,
        ).start()

    pltpu.make_async_copy(mass_in, mass_in, mass_recv).wait()
    result = result + jnp.sum(mass_in[...], axis=0)
    projected[...] = result

    for it in range(ITERS):
        pltpu.make_async_copy(row_in.at[it], row_in.at[it], row_send.at[it]).wait()
        rest = potential.at[it, :, pl.ds(0, n_i - piece)]
        pltpu.make_async_copy(rest, rest, pot_send.at[it]).wait()
        pltpu.make_async_copy(col_in.at[it], col_in.at[it], col_send.at[it]).wait()
    pltpu.make_async_copy(mass_in, mass_in, mass_send).wait()


def solution(mesh):
    return local(mesh, mesh.shape["src"], mesh.shape["tgt"])


def local(mesh, n_src, n_tgt, comm=True):
    def per_device(xs, ys, a_mass, b_mass, s_region, t_region, allowed):
        width, n_i = xs.shape
        n_j = ys.shape[1]
        share = width // n_src
        tiles = n_i // TILE
        half = tiles // 2
        chips = n_tgt // 2
        piece = n_i // n_tgt
        vmem = pl.BlockSpec(memory_space=pltpu.VMEM)
        smem = pl.BlockSpec(memory_space=pltpu.SMEM)
        hbm = pl.BlockSpec(memory_space=pltpu.HBM)
        dma = pltpu.SemaphoreType.DMA

        def call(body, first, b_mass, s_region, t_region, f_shape, g_shape, scratch, identity):
            spare = (
                jax.ShapeDtypeStruct(g_shape, F32),
                jax.ShapeDtypeStruct((1,), jnp.int32),
                jax.ShapeDtypeStruct(s_region.shape, jnp.int32),
                jax.ShapeDtypeStruct(t_region.shape, jnp.int32),
            )
            return pl.pallas_call(
                functools.partial(body, n_src=n_src, n_tgt=n_tgt),
                out_shape=(
                    jax.ShapeDtypeStruct(f_shape, F32),
                    jax.ShapeDtypeStruct(g_shape, F32),
                    jax.ShapeDtypeStruct((share, n_j), F32),
                )
                + spare * first,
                in_specs=[hbm] * 7 if first else [vmem] * 4 + [smem] * 3,
                out_specs=(vmem, vmem, vmem) + (vmem, smem, smem, smem) * first,
                scratch_shapes=scratch,
                compiler_params=pltpu.CompilerParams(
                    collective_id=identity if comm else None,
                    has_side_effects=comm,
                    vmem_limit_bytes=VMEM_MIB * 1024 * 1024,
                ),
            )(xs, ys, a_mass.reshape(f_shape), b_mass.reshape(g_shape), s_region, t_region, allowed)

        f, g, projected, b_copy, failed, s_copy, t_copy = call(
            functools.partial(kernel, comm=comm), 1, b_mass, s_region, t_region, (n_i // LANES, LANES), (n_j // LANES, LANES),
            [
                pltpu.VMEM((width, n_j), BF16),
                pltpu.VMEM((n_i // LANES, LANES), F32),
                pltpu.VMEM((n_j // LANES, LANES), F32),
                pltpu.SMEM(s_region.shape, jnp.int32),
                pltpu.SMEM(t_region.shape, jnp.int32),
                pltpu.SMEM(allowed.shape, jnp.int32),
                pltpu.VMEM((256, n_i), BF16),
                pltpu.VMEM((256, n_j), BF16),
                pltpu.VMEM((n_j, 256), BF16),
                pltpu.VMEM((n_i, 128), BF16),
                pltpu.VMEM((n_j // LANES, LANES), F32),
                pltpu.VMEM((n_j, n_i), F32),
                pltpu.VMEM((n_j, LANES), F32),
                pltpu.VMEM((n_j, LANES), F32),
                pltpu.VMEM((n_i // LANES, LANES), F32),
                pltpu.VMEM((half, 8, LANES), F32),
                pltpu.VMEM((ITERS, half, 8, LANES), F32),
                pltpu.VMEM((ITERS, half, 8, LANES), F32),
                pltpu.VMEM((ITERS, half, chips, 8, LANES), F32),
                pltpu.VMEM((ITERS, half, 8, LANES), F32),
                pltpu.VMEM((ITERS, half, 8, LANES), F32),
                pltpu.VMEM((ITERS, n_src, 8, LANES), F32),
                pltpu.VMEM((n_j, LANES), F32),
                pltpu.VMEM((n_src, share, n_j), F32),
                pltpu.VMEM((n_src, share, n_j), F32),
                dma((9,)),
                *[dma((ITERS, half))] * 6,
                dma((ITERS,)), dma((ITERS,)), dma, dma,
            ],
            0,
        )
        f, g = f.reshape(n_i), g.reshape(n_j)
        if not comm:
            return f, g, projected

        def careful():
            f, g, projected = call(
                careful_kernel, 0, b_copy, s_copy, t_copy, (1, n_i), (1, n_j),
                [
                    pltpu.VMEM((256, n_i), BF16),
                    pltpu.VMEM((256, n_j), BF16),
                    pltpu.VMEM((n_i, 256), BF16),
                    pltpu.VMEM((n_j, 256), BF16),
                    pltpu.VMEM((ITERS, 1, n_i), F32),
                    pltpu.VMEM((ITERS, 1, n_j), F32),
                    pltpu.VMEM((n_src, share, n_j), F32),
                    pltpu.VMEM((ITERS, n_tgt - 1, 1, piece), F32),
                    pltpu.VMEM((ITERS, 1, n_i), F32),
                    pltpu.VMEM((ITERS, n_src - 1, 1, n_j), F32),
                    pltpu.VMEM((n_src - 1, share, n_j), F32),
                    dma((ITERS,)), dma((ITERS,)), dma((ITERS,)), dma((ITERS,)),
                    dma((ITERS,)), dma((ITERS,)), dma, dma,
                ],
                1,
            )
            return f.reshape(n_i), g.reshape(n_j), projected

        return lax.cond(failed[0] > 0, careful, lambda: (f, g, projected))

    placed = (P(None, "src"), P(None, "tgt"), P("src"), P("tgt"), P("src"), P("tgt"), P())
    return jax.shard_map(
        per_device,
        mesh=mesh,
        in_specs=placed,
        out_specs=(P("src"), P("tgt"), P("src", "tgt")),
        check_vma=False,
    )
```
